256 devices in a mesh: ham: 32 (over z, y_hi, core), walk: 8 (over x, y_lo).
Axes of the slice: x: 4, y: 4 (y_hi: 2, y_lo: 2; y = y_hi * 2 + y_lo), z: 8, core: 2. Of those that a mesh axis runs over, the one named last changes fastest.
Arguments:
- chol: bfloat16 [128, 256, 1024], P('ham'), may hold values from -0.1875 to 0.1875
- green: bfloat16 [1024, 1024, 256], P(('walk', 'ham')), may hold values from -6 to 6
- fields: float32 [1024, 16], P(('walk', 'ham')), may hold values from -5 to 5
- weights_in: float32 [1024], P(('walk', 'ham')), may hold values from 0.5 to 2
- partner: int32 [1024], P(('walk', 'ham')), may hold values from 0 to 1023, as said below
- counts: int32 [8, 32], P('walk', 'ham'), may hold values from 1 to 4, as said below
Outputs:
- paired_weights: float32 [1024], P(('walk', 'ham'))
- local_energy: float32 [1024], P(('walk', 'ham'))
- force_bias: float32 [1024, 16], P(('walk', 'ham'))
- energy_mean: float32 [], replicated
The draws below stay inside these ranges and needn't reach their ends.
Inputs may be any that keep to these rules, and one draw needn't show every extreme that they name: partner[partner[w]] = w; partner[w] lies in another group than w, at the same slab position (w // 4) % 32; all walkers of one group are matched into one group. `counts`: some entry equals 4.
All inputs are finite; a program needn't handle non-finite values.
Results may differ from the reference program's by a relative error of at most 0.0003.
Values may be sent and summed in bfloat16 or wider, within the bound.
A program may use at most 128 MiB of HBM per device.

```python
import math
import jax
import jax.numpy as jnp
from jax import lax

ORB = 1024
NOCC = 256
CHOL_DEV = 4
WALK_DEV = 4
STOPS = 4
NCHOL = 128
WALKERS = 1024
N_HAM = 32
N_WALK = 8


def draw_partner(key, part):
    key = jax.random.fold_in(key, 11)
    first, second = jax.random.split(key)
    order = jax.random.permutation(first, N_WALK)
    place = jnp.argsort(order, stable=True)
    mate_group = order[jnp.bitwise_xor(place, 1)].astype(jnp.int32)
    scores = jax.random.randint(second, (N_WALK, N_HAM, WALK_DEV), 0, 65536) * WALK_DEV + jnp.arange(WALK_DEV, dtype=jnp.int32)
    sigma = jnp.argsort(scores, axis=-1, stable=True).astype(jnp.int32)
    inverse = jnp.argsort(sigma, axis=-1, stable=True).astype(jnp.int32)
    group_ids = jnp.arange(N_WALK, dtype=jnp.int32)
    lower = (group_ids < mate_group)[:, None, None]
    local = jnp.where(lower, sigma, inverse[mate_group])
    blocks = jnp.arange(N_HAM, dtype=jnp.int32)[None, :, None]
    result = mate_group[:, None, None] * (N_HAM * WALK_DEV) + blocks * WALK_DEV + local
    return result.reshape(N_WALK * N_HAM * WALK_DEV).astype(jnp.int32)


def draw_counts(key, part):
    key = jax.random.fold_in(key, 23)
    first, second = jax.random.split(key)
    values = jax.random.randint(first, (N_WALK * N_HAM,), 1, WALK_DEV + 1)
    order = jax.random.permutation(second, N_WALK * N_HAM)
    values = values.at[order[0]].set(WALK_DEV)
    return values.reshape(N_WALK, N_HAM).astype(jnp.int32)


def shard_levels(stream_key, shape, cuts, smallest, top_value):
    gain, own = 1.0, jax.random.fold_in(stream_key, 6)
    for position, shards_of in cuts:
        steps = jnp.exp(jax.random.uniform(jax.random.fold_in(own, position), (shards_of,), jnp.float32, smallest / len(cuts), top_value / len(cuts)))
        gain = gain * jnp.repeat(steps, shape[position] // shards_of).reshape([-1 if axis == position else 1 for axis in range(len(shape))])
    return gain


def scatter_about(rng, shape, spread, bound, shards=(), held_as=jnp.bfloat16):
    array = jax.random.normal(rng, shape, jnp.float32) * spread
    if len(shards) > 0:
        array = shard_levels(rng, shape, shards, -0.22, 0.18) * array
    return jnp.clip(array, min=-bound, max=bound).astype(held_as)


def setup_inputs(seed: int = 0) -> dict:
    seeds = jax.random.split(jax.random.key(seed), 7)
    chol = scatter_about(seeds[0], (NCHOL, NOCC, ORB), ORB ** -0.5, 0.1875, ((0, 32),))
    green = scatter_about(seeds[1], (WALKERS, ORB, NOCC), 1.0, 6.0, ((0, 256),))
    fields = scatter_about(seeds[2], (WALKERS, STOPS * CHOL_DEV), 1.0, 5.0, ((0, 256),), jnp.float32)
    weights_in = jnp.clip(jnp.exp(math.log(2.0) - 1.3862944 * jax.random.uniform(seeds[3], (WALKERS,), jnp.float32) ** shard_levels(seeds[3], (WALKERS,), ((0, 256),), -0.2, 0.2)), 0.5, 2.0)
    partner = draw_partner(jax.random.fold_in(seeds[6], 71), 0)
    counts = draw_counts(jax.random.fold_in(seeds[6], 71), 0)
    return dict(chol=chol, green=green, fields=fields, weights_in=weights_in, partner=partner, counts=counts)


FIELD_COUPLING = 0.02
DRIFT_COST = 0.0002
ONE_BODY = 1.0


def stop_terms(slabs, theta):
    prod = jnp.einsum('svik,bkj->bsvij', slabs, theta)
    bias_part = jnp.trace(prod, axis1=3, axis2=4)
    exchange_part = jnp.sum(prod * jnp.swapaxes(prod, 3, 4), axis=(1, 2, 3, 4))
    return bias_part, exchange_part


def reference(chol, green, fields, weights_in, partner, counts):
    slabs = chol.astype(jnp.float32).reshape(N_HAM, CHOL_DEV, NOCC, ORB)
    thetas = green.astype(jnp.float32).reshape(N_WALK, N_HAM, WALK_DEV, ORB, NOCC)
    thetas = thetas.transpose(1, 0, 2, 3, 4).reshape(N_HAM, N_WALK * WALK_DEV, ORB, NOCC)
    visited = jnp.stack([jnp.roll(slabs, -offset, axis=0) for offset in range(-1, STOPS - 1)], axis=1)
    bias_all, exchange_all = lax.map(lambda pair: stop_terms(pair[0], pair[1]), (visited, thetas))
    force_bias = bias_all.reshape(N_HAM, N_WALK, WALK_DEV, STOPS * CHOL_DEV).transpose(1, 0, 2, 3).reshape(WALKERS, STOPS * CHOL_DEV)
    exchange = exchange_all.reshape(N_HAM, N_WALK, WALK_DEV).transpose(1, 0, 2).reshape(WALKERS)
    squares = jnp.sum(force_bias * force_bias, axis=1)
    local_energy = ONE_BODY + (0.5 * squares - 0.5 * exchange) / (NOCC * STOPS * CHOL_DEV)
    index = jnp.arange(WALKERS)
    flat_counts = counts.reshape(N_WALK * N_HAM)
    live = (index % WALK_DEV < flat_counts[index // WALK_DEV]).astype(jnp.float32)
    log_ratio = FIELD_COUPLING * jnp.sum(fields * force_bias, axis=1) - DRIFT_COST * squares
    new_weight = weights_in * jnp.exp(log_ratio) * live
    paired_weights = 0.5 * (new_weight + new_weight[partner])
    energy_mean = jnp.sum(new_weight * local_energy) / jnp.sum(new_weight)
    return paired_weights, local_energy, force_bias, energy_mean
```

```python
import jax
import jax.numpy as jnp
from jax import lax
from jax.experimental import pallas as pl
from jax.experimental.pallas import tpu as pltpu
from jax.sharding import PartitionSpec as P

ORB = 1024
NOCC = 256
VECS = 4
STOPS = 4
WALKERS_DEV = 4
QUARTER = NOCC // 4
EIGHTH = NOCC // 8
FIELD_COUPLING = 0.02
DRIFT_COST = 0.0002
ONE_BODY = 1.0
MESH = pl.DeviceIdType.MESH
LANES = 128
EXCH_LANE = 16
WEIGHT_LANE = 17
LIVE_LANE = 18


def product_terms(prod):
    a, b = prod[:128, :128], prod[:128, 128:]
    c, d = prod[128:, :128], prod[128:, 128:]
    i = lax.broadcasted_iota(jnp.int32, (128, 128), 0)
    j = lax.broadcasted_iota(jnp.int32, (128, 128), 1)
    low = jnp.where(i >= j, a, d)
    high = jnp.where(i < j, a, d)
    pairs = high * low.T + b * c.T
    gap = jnp.where(i == j, a - d, 0.0)
    diag = jnp.where(i == j, a + d, 0.0)
    exchange = jnp.sum((pairs + pairs + gap * gap).reshape(16, 8, 128), axis=0)
    trace = jnp.sum(diag, axis=0, keepdims=True)
    return trace, exchange


def kernel(
    chol, green, fields, weights, partner, counts, out,
    slab, theta, far, transit, trace, exch, meta, meta_in, bias, bias_in, plane, line,
    load_sem, theta_sem, meta_sem, bias_sem, entry_send, entry_recv, transit_send, transit_recv,
    share_send, share_recv, direct_send, direct_recv, plane_sem, line_sem,
):
    h, g = lax.axis_index("ham"), lax.axis_index("walk")
    z, y_hi, core = h // 4, lax.rem(h // 2, 2), lax.rem(h, 2)
    x, y_lo = g // 2, lax.rem(g, 2)
    y = y_hi * 2 + y_lo

    def device(x=x, y_hi=y_hi, y_lo=y_lo, z=z, core=core):
        return {"ham": z * 4 + y_hi * 2 + core, "walk": x * 2 + y_lo}

    sibling = device(core=1 - core)
    cross = device(y_hi=1 - y_hi, y_lo=1 - y_lo)
    twin = device(y_lo=1 - y_lo)
    x_up, x_down = device(x=lax.rem(x + 1, 4)), device(x=lax.rem(x + 3, 4))
    z_down = device(z=lax.rem(z + 7, 8))
    z_on = device(z=lax.rem(z + 9 - 2 * y_hi, 8))
    sharers = (x_down, x_up, twin)
    color = lax.rem(x + 2 * y_lo, 4)
    cross_color = lax.rem(x + 2 * (1 - y_lo), 4)
    colors = (lax.rem(color + 1, 4), lax.rem(color + 3, 4), lax.rem(color + 2, 4))

    def plane_peer(d):
        yy = lax.rem(y + d // 4, 4)
        return device(x=lax.rem(x + d % 4, 4), y_hi=yy // 2, y_lo=lax.rem(yy, 2))

    def line_peer(d):
        return device(z=lax.rem(z + d, 8))

    def quarter(k):
        return pl.ds(pl.multiple_of(k * QUARTER, QUARTER), QUARTER)

    def first(k):
        return pl.ds(pl.multiple_of(k * QUARTER, EIGHTH), EIGHTH)

    def second(k):
        return pl.ds(pl.multiple_of(k * QUARTER + EIGHTH, EIGHTH), EIGHTH)

    def remote(src, dst, send, recv, to):
        return pltpu.make_async_remote_copy(src, dst, send, recv, device_id=to, device_id_type=MESH)

    barrier = pltpu.get_barrier_semaphore()
    pl.semaphore_signal(barrier, inc=1, device_id=sibling, device_id_type=MESH)
    for d in range(1, 16):
        pl.semaphore_signal(barrier, inc=1, device_id=plane_peer(d), device_id_type=MESH)
    for d in range(1, 8):
        pl.semaphore_signal(barrier, inc=1, device_id=line_peer(d), device_id_type=MESH)

    own_rows = pl.ds(core * WALKERS_DEV, WALKERS_DEV)
    load_slab = pltpu.make_async_copy(chol, slab, load_sem.at[0])
    load_theta = pltpu.make_async_copy(green, theta.at[own_rows], load_sem.at[1])
    load_slab.start()
    load_theta.start()
    row = lax.broadcasted_iota(jnp.int32, (8, LANES), 0)
    lane = lax.broadcasted_iota(jnp.int32, (8, LANES), 1)
    mine = row // 4 == core
    meta[...] = jnp.zeros_like(meta)
    meta[0:4, 0:16] = fields[...]
    meta[4:8, 0:16] = fields[...]
    values = meta[...]
    for i in range(WALKERS_DEV):
        values = jnp.where((row % 4 == i) & (lane == WEIGHT_LANE), weights[i], values)
    values = jnp.where((row % 4 < counts[0, 0]) & (lane == LIVE_LANE), 1.0, values)
    meta[...] = jnp.where(mine, values, 0.0)
    exch[...] = jnp.zeros_like(exch)

    pl.semaphore_wait(barrier, 23)

    swap_theta = remote(green, theta.at[own_rows], theta_sem.at[0], theta_sem.at[1], sibling)
    swap_meta = remote(meta, meta_in, meta_sem.at[0], meta_sem.at[1], sibling)

    def entry_out(src, v):
        return remote(src, far.at[0, v, quarter(cross_color)], entry_send.at[0, v], entry_recv.at[0, v], cross)

    def entry_in(s, v):
        rows = far.at[s, v, quarter(color)]
        return remote(rows, rows, entry_send.at[s, v], entry_recv.at[s, v], cross)

    def entry_on(v):
        rows = far.at[0, v, quarter(color)]
        return remote(rows, far.at[1, v, quarter(color)], entry_send.at[1, v], entry_recv.at[1, v], z_on)

    def transit_copy(v):
        return remote(chol.at[v, quarter(cross_color)], transit.at[v], transit_send.at[v], transit_recv.at[v], z_down)

    def part(s, k):
        return quarter(k) if s == 0 else first(k)

    def share_out(s, v, n):
        rows = far.at[s, v, part(s, color)]
        return remote(rows, rows, share_send.at[s, v, n], share_recv.at[s, v, n], sharers[n])

    def share_in(s, v, n):
        rows = far.at[s, v, part(s, colors[n])]
        return remote(rows, rows, share_send.at[s, v, n], share_recv.at[s, v, n], sharers[n])

    def direct(v, n):
        rows = second(colors[n])
        return remote(far.at[0, v, rows], far.at[1, v, rows], direct_send.at[v, n], direct_recv.at[v, n], z_on)

    def note(slot, w, terms):
        trace[slot, pl.ds(w, 1), :] = terms[0]
        exch[w] += terms[1]

    def own_step(w):
        prod = jnp.dot(slab[...].reshape(VECS * NOCC, ORB), theta[w], preferred_element_type=jnp.float32)
        for v in range(VECS):
            note(v, w, product_terms(prod[v * NOCC:(v + 1) * NOCC]))

    def far_step(s, v, base, count):
        vector = far[s, v]
        for n in range(count):
            w = base + n
            prod = jnp.dot(vector, theta[w], preferred_element_type=jnp.float32)
            note(VECS + v, w, product_terms(prod))

    def own_pair(v, n):
        base = jnp.where(v < 2, core, 1 - core) * WALKERS_DEV + lax.rem(v, 2) * 2
        own_step(base + n)

    @pl.when(core == 0)
    def _():
        @pl.when(y_hi == 0)
        def _():
            for v in range(VECS):
                transit_copy(v).start()

        @pl.when(y_hi == 1)
        def _():
            for v in range(VECS):
                entry_out(chol.at[v, quarter(cross_color)], v).start()

        swap_theta.start()
        swap_meta.start()
        load_slab.wait()
        load_theta.wait()

        def round_(v, carry):
            @pl.when(y_hi == 0)
            def _():
                transit_copy(v).wait_recv()
                entry_out(transit.at[v], v).start()

            own_pair(v, 0)
            entry_in(0, v).wait_recv()
            for n in range(3):
                share_out(0, v, n).start()

            @pl.when(v == 1)
            def _():
                swap_theta.wait_recv()

            own_pair(v, 1)

            @pl.when(v > 0)
            def _():
                for n in range(3):
                    share_in(0, v - 1, n).wait_recv()
                far_step(0, v - 1, 0, 8)

            return carry

        lax.fori_loop(0, VECS, round_, 0)
        for n in range(3):
            share_in(0, VECS - 1, n).wait_recv()
        far_step(0, VECS - 1, 0, 8)

    @pl.when(core == 1)
    def _():
        for v in range(VECS):
            entry_out(chol.at[v, quarter(cross_color)], v).start()
        swap_theta.start()
        swap_meta.start()
        load_slab.wait()
        load_theta.wait()
        near_base = (1 - y_hi) * WALKERS_DEV
        next_base = y_hi * WALKERS_DEV

        def finish(v):
            for n in range(3):
                share_in(1, v, n).wait_recv()
                direct(v, n).wait_recv()
            far_step(1, v, next_base, 4)

        def round_(v, carry):
            own_pair(v, 0)
            entry_in(0, v).wait_recv()
            for n in range(3):
                share_out(0, v, n).start()
            entry_on(v).start()

            own_pair(v, 1)

            @pl.when(v == 0)
            def _():
                swap_theta.wait_recv()

            for n in range(3):
                share_in(0, v, n).wait_recv()
                direct(v, n).start()
            entry_in(1, v).wait_recv()
            for n in range(3):
                share_out(1, v, n).start()
            far_step(0, v, near_base, 4)

            @pl.when(v > 0)
            def _():
                finish(v - 1)

            return carry

        lax.fori_loop(0, VECS, round_, 0)
        finish(VECS - 1)

    lower = row < 4
    tile = jnp.zeros((8, LANES), jnp.float32)
    own_cols = jnp.where(lower, 4 + 4 * core, 4 * core)
    far_cols = jnp.where(lower, 12 - 12 * core, 8 + 4 * core)
    for slot in range(2 * VECS):
        cols = own_cols if slot < VECS else far_cols
        total = jnp.sum(trace[slot], axis=1, keepdims=True)
        tile = jnp.where(lane == cols + slot % VECS, total, tile)
    exch_rows = jnp.sum(exch[...], axis=1)
    tile = jnp.where(lane == EXCH_LANE, jnp.sum(exch_rows, axis=1, keepdims=True), tile)
    bias[...] = tile
    swap_bias = remote(bias, bias_in, bias_sem.at[0], bias_sem.at[1], sibling)
    swap_bias.start()
    swap_meta.wait_recv()
    known = meta[...] + meta_in[...]
    swap_bias.wait_recv()
    full = bias[...] + bias_in[...]
    is_bias = lane < STOPS * VECS

    def pick(keep, values):
        return jnp.sum(jnp.where(keep, values, 0.0), axis=1, keepdims=True)

    squares = pick(is_bias, full * full)
    drift = pick(is_bias, full * known)
    exchange = pick(lane == EXCH_LANE, full)
    energy = ONE_BODY + (0.5 * squares - 0.5 * exchange) / (NOCC * STOPS * VECS)
    weight = pick(lane == WEIGHT_LANE, known) * pick(lane == LIVE_LANE, known)
    weight = weight * jnp.exp(FIELD_COUPLING * drift - DRIFT_COST * squares)
    here = jnp.where(lane == 0, weight, jnp.where(lane == 1, weight * energy, 0.0))

    my_plane = x * 4 + y
    plane[my_plane] = here
    for d in range(1, 16):
        remote(plane.at[my_plane], plane.at[my_plane], plane_sem.at[0], plane_sem.at[1], plane_peer(d)).start()
    some = plane.at[pl.ds(0, 15)]
    remote(some, some, plane_sem.at[0], plane_sem.at[1], sibling).wait_recv()
    summed = plane[0]
    for n in range(1, 16):
        summed = summed + plane[n]
    line[z] = summed
    for d in range(1, 8):
        remote(line.at[z], line.at[z], line_sem.at[0], line_sem.at[1], line_peer(d)).start()

    table = jnp.zeros((8, LANES), jnp.float32)
    for n in range(8):
        column = plane[(n // 2) * 4 + y_hi * 2 + n % 2]
        table = jnp.where(lane == n, pick(lane == 0, column), table)
    mate = jnp.zeros((8, LANES), jnp.float32)
    for i in range(WALKERS_DEV):
        found = (row == core * 4 + (partner[i] & 3)) & (lane == partner[i] // (WALKERS_DEV * 32))
        value = jnp.sum(pick(found, table), axis=0, keepdims=True)
        mate = jnp.where(row % 4 == i, value, mate)
    paired = 0.5 * (weight + mate)

    some_line = line.at[pl.ds(0, 7)]
    remote(some_line, some_line, line_sem.at[0], line_sem.at[1], sibling).wait_recv()
    summed = line[0]
    for n in range(1, 8):
        summed = summed + line[n]
    totals = jnp.sum(summed, axis=0, keepdims=True)
    top = jnp.broadcast_to(totals, (8, LANES))
    mean = pick(lane == 1, top) / pick(lane == 0, top)
    result = jnp.where(is_bias, full, 0.0)
    result = jnp.where(lane == 16, paired, result)
    result = jnp.where(lane == 17, energy, result)
    result = jnp.where(lane == 18, mean, result)
    out[...] = jnp.where(core == 0, result[0:4], result[4:8])

    remote(some, some, plane_sem.at[0], plane_sem.at[1], sibling).wait_send()
    remote(some_line, some_line, line_sem.at[0], line_sem.at[1], sibling).wait_send()
    swap_bias.wait_send()
    swap_theta.wait_send()
    swap_meta.wait_send()

    def sent(v, carry):
        for n in range(3):
            share_out(0, v, n).wait_send()

        @pl.when(core == 0)
        def _():
            @pl.when(y_hi == 0)
            def _():
                transit_copy(v).wait_send()

        entry_out(transit.at[v], v).wait_send()

        @pl.when(core == 1)
        def _():
            entry_on(v).wait_send()
            for n in range(3):
                share_out(1, v, n).wait_send()
                direct(v, n).wait_send()

        return carry

    lax.fori_loop(0, VECS, sent, 0)


def body(chol, green, fields, weights_in, partner, counts):
    anywhere = pl.BlockSpec(memory_space=pl.ANY)
    vmem = pl.BlockSpec(memory_space=pltpu.VMEM)
    smem = pl.BlockSpec(memory_space=pltpu.SMEM)
    dma = pltpu.SemaphoreType.DMA
    tile = pltpu.VMEM((8, LANES), jnp.float32)
    out = pl.pallas_call(
        kernel,
        out_shape=jax.ShapeDtypeStruct((4, LANES), jnp.float32),
        in_specs=[anywhere, anywhere, vmem, smem, smem, smem],
        out_specs=vmem,
        scratch_shapes=[
            pltpu.VMEM((VECS, NOCC, ORB), jnp.bfloat16),
            pltpu.VMEM((2 * WALKERS_DEV, ORB, NOCC), jnp.bfloat16),
            pltpu.VMEM((2, VECS, NOCC, ORB), jnp.bfloat16),
            pltpu.VMEM((VECS, QUARTER, ORB), jnp.bfloat16),
            pltpu.VMEM((2 * VECS, 8, LANES), jnp.float32),
            pltpu.VMEM((8, 8, LANES), jnp.float32),
            tile, tile, tile, tile,
            pltpu.VMEM((16, 8, LANES), jnp.float32),
            pltpu.VMEM((8, 8, LANES), jnp.float32),
            dma((2,)), dma((2,)), dma((2,)), dma((2,)),
            dma((2, VECS)), dma((2, VECS)), dma((VECS,)), dma((VECS,)),
            dma((2, VECS, 3)), dma((2, VECS, 3)), dma((VECS, 3)), dma((VECS, 3)),
            dma((2,)), dma((2,)),
        ],
        compiler_params=pltpu.CompilerParams(
            collective_id=0, has_side_effects=True, vmem_limit_bytes=48 * 2**20
        ),
        name="walkers",
    )(chol, green, fields, weights_in, partner, counts)
    return out[:, 16], out[:, 17], out[:, : STOPS * VECS], out[0, 18]


def solution(mesh):
    placed = (
        P("ham", None, None),
        P(("walk", "ham"), None, None),
        P(("walk", "ham"), None),
        P(("walk", "ham")),
        P(("walk", "ham")),
        P("walk", "ham"),
    )
    return jax.shard_map(
        body,
        mesh=mesh,
        in_specs=placed,
        out_specs=(P(("walk", "ham")), P(("walk", "ham")), P(("walk", "ham"), None), P()),
        check_vma=False,
    )
```

```python
import jax
import jax.numpy as jnp
from jax import lax
from jax.experimental import pallas as pl
from jax.experimental.pallas import tpu as pltpu
from jax.sharding import PartitionSpec as P

ORB = 1024
NOCC = 256
VECS = 4
STOPS = 4
WALKERS_DEV = 4
QUARTER = NOCC // 4
EIGHTH = NOCC // 8
FIELD_COUPLING = 0.02
DRIFT_COST = 0.0002
ONE_BODY = 1.0
MESH = pl.DeviceIdType.MESH
LANES = 128
EXCH_LANE = 16
WEIGHT_LANE = 17
LIVE_LANE = 18
PLAN_0 = (
    "o0", "o1", "o2", "o3", "t0", "o4", "t1", "o5", "t2", "o6", "t3", "o7",
    "e0", "e1", "e2", "s0", "a0", "e3", "s1", "a1", "s2", "a2", "s3", "a3",
)
PLAN_1 = (
    "o0", "o1", "o2", "e0", "o3", "e1", "e2", "o4", "e3", "s0", "f0", "o5",
    "s1", "f1", "p0", "s2", "f2", "o6", "s3", "f3", "o7", "g0", "q0", "p1",
    "g1", "q1", "p2", "g2", "q2", "p3", "g3", "q3",
)


def product_terms(prod):
    a, b = prod[:128, :128], prod[:128, 128:]
    c, d = prod[128:, :128], prod[128:, 128:]
    i = lax.broadcasted_iota(jnp.int32, (128, 128), 0)
    j = lax.broadcasted_iota(jnp.int32, (128, 128), 1)
    low = jnp.where(i >= j, a, d)
    high = jnp.where(i < j, a, d)
    pairs = high * low.T + b * c.T
    gap = jnp.where(i == j, a - d, 0.0)
    diag = jnp.where(i == j, a + d, 0.0)
    exchange = jnp.sum((pairs + pairs + gap * gap).reshape(16, 8, 128), axis=0)
    trace = jnp.sum(diag, axis=0, keepdims=True)
    return trace, exchange


def kernel(
    chol, green, fields_in, weights_in, partner_in, counts_in, out,
    fields, weights, partner, counts, slab, theta, far, transit, trace, exch, meta, meta_in, bias, bias_in, plane, line,
    small_sem, load_sem, theta_sem, meta_sem, bias_sem, entry_send, entry_recv, transit_send, transit_recv,
    share_send, share_recv, direct_send, direct_recv, plane_sem, line_sem,
):
    h, g = lax.axis_index("ham"), lax.axis_index("walk")
    z, y_hi, core = h // 4, lax.rem(h // 2, 2), lax.rem(h, 2)
    x, y_lo = g // 2, lax.rem(g, 2)
    y = y_hi * 2 + y_lo

    def device(x=x, y_hi=y_hi, y_lo=y_lo, z=z, core=core):
        return {"ham": z * 4 + y_hi * 2 + core, "walk": x * 2 + y_lo}

    sibling = device(core=1 - core)
    cross = device(y_hi=1 - y_hi, y_lo=1 - y_lo)
    twin = device(y_lo=1 - y_lo)
    x_up, x_down = device(x=lax.rem(x + 1, 4)), device(x=lax.rem(x + 3, 4))
    z_down = device(z=lax.rem(z + 7, 8))
    z_on = device(z=lax.rem(z + 9 - 2 * y_hi, 8))
    sharers = (x_down, x_up, twin)
    color = lax.rem(x + 2 * y_lo, 4)
    cross_color = lax.rem(x + 2 * (1 - y_lo), 4)
    colors = (lax.rem(color + 1, 4), lax.rem(color + 3, 4), lax.rem(color + 2, 4))

    def plane_peer(d):
        yy = lax.rem(y + d // 4, 4)
        return device(x=lax.rem(x + d % 4, 4), y_hi=yy // 2, y_lo=lax.rem(yy, 2))

    def line_peer(d):
        return device(z=lax.rem(z + d, 8))

    def quarter(k):
        return pl.ds(pl.multiple_of(k * QUARTER, QUARTER), QUARTER)

    def first(k):
        return pl.ds(pl.multiple_of(k * QUARTER, EIGHTH), EIGHTH)

    def second(k):
        return pl.ds(pl.multiple_of(k * QUARTER + EIGHTH, EIGHTH), EIGHTH)

    def remote(src, dst, send, recv, to):
        return pltpu.make_async_remote_copy(src, dst, send, recv, device_id=to, device_id_type=MESH)

    own_rows = pl.ds(core * WALKERS_DEV, WALKERS_DEV)
    small = [
        pltpu.make_async_copy(src, dst, small_sem.at[n])
        for n, (src, dst) in enumerate(
            ((fields_in, fields), (weights_in, weights), (partner_in, partner), (counts_in, counts))
        )
    ]
    for copy in small:
        copy.start()
    load_slab = pltpu.make_async_copy(chol, slab, load_sem.at[0])
    load_theta = pltpu.make_async_copy(green, theta.at[own_rows], load_sem.at[1])
    load_slab.start()
    load_theta.start()

    barrier = pltpu.get_barrier_semaphore()
    pl.semaphore_signal(barrier, inc=1, device_id=sibling, device_id_type=MESH)
    for d in range(1, 16):
        pl.semaphore_signal(barrier, inc=1, device_id=plane_peer(d), device_id_type=MESH)
    for d in range(1, 8):
        pl.semaphore_signal(barrier, inc=1, device_id=line_peer(d), device_id_type=MESH)

    for copy in small:
        copy.wait()
    row = lax.broadcasted_iota(jnp.int32, (8, LANES), 0)
    lane = lax.broadcasted_iota(jnp.int32, (8, LANES), 1)
    mine = row // 4 == core
    meta[...] = jnp.zeros_like(meta)
    meta[0:4, 0:16] = fields[...]
    meta[4:8, 0:16] = fields[...]
    values = meta[...]
    for i in range(WALKERS_DEV):
        values = jnp.where((row % 4 == i) & (lane == WEIGHT_LANE), weights[i], values)
    values = jnp.where((row % 4 < counts[0, 0]) & (lane == LIVE_LANE), 1.0, values)
    meta[...] = jnp.where(mine, values, 0.0)
    exch[...] = jnp.zeros_like(exch)

    load_slab.wait()
    load_theta.wait()
    pl.semaphore_wait(barrier, 23)

    swap_theta = remote(theta.at[own_rows], theta.at[own_rows], theta_sem.at[0], theta_sem.at[1], sibling)
    swap_meta = remote(meta, meta_in, meta_sem.at[0], meta_sem.at[1], sibling)

    def entry_out(src, v):
        return remote(src, far.at[0, v, quarter(cross_color)], entry_send.at[0, v], entry_recv.at[0, v], cross)

    def entry_in(s, v):
        rows = far.at[s, v, quarter(color)]
        return remote(rows, rows, entry_send.at[s, v], entry_recv.at[s, v], cross)

    def entry_on(v):
        rows = far.at[0, v, quarter(color)]
        return remote(rows, far.at[1, v, quarter(color)], entry_send.at[1, v], entry_recv.at[1, v], z_on)

    def transit_copy(v):
        return remote(slab.at[v, quarter(cross_color)], transit.at[v], transit_send.at[v], transit_recv.at[v], z_down)

    def part(s, k):
        return quarter(k) if s == 0 else first(k)

    def share_out(s, v, n):
        rows = far.at[s, v, part(s, color)]
        return remote(rows, rows, share_send.at[s, v, n], share_recv.at[s, v, n], sharers[n])

    def share_in(s, v, n):
        rows = far.at[s, v, part(s, colors[n])]
        return remote(rows, rows, share_send.at[s, v, n], share_recv.at[s, v, n], sharers[n])

    def direct(v, n):
        rows = second(colors[n])
        return remote(far.at[0, v, rows], far.at[1, v, rows], direct_send.at[v, n], direct_recv.at[v, n], z_on)

    def note(slot, w, terms):
        trace[slot, pl.ds(w, 1), :] = terms[0]
        exch[w] += terms[1]

    def own_step(w):
        prod = jnp.dot(slab[...].reshape(VECS * NOCC, ORB), theta[w], preferred_element_type=jnp.float32)
        for v in range(VECS):
            note(v, w, product_terms(prod[v * NOCC:(v + 1) * NOCC]))

    def far_step(s, v, base, count):
        vector = far[s, v]
        for n in range(count):
            w = base + n
            prod = jnp.dot(vector, theta[w], preferred_element_type=jnp.float32)
            note(VECS + v, w, product_terms(prod))

    near_base = (1 - y_hi) * WALKERS_DEV
    next_base = y_hi * WALKERS_DEV

    def pass_on(v):
        @pl.when(y_hi == 0)
        def _():
            transit_copy(v).wait_recv()
            entry_out(transit.at[v], v).start()

        @pl.when(y_hi == 1)
        def _():
            entry_out(slab.at[v, quarter(cross_color)], v).start()

    def enter(v):
        entry_in(0, v).wait_recv()
        for n in range(3):
            share_out(0, v, n).start()

    def enter_on(v):
        entry_in(0, v).wait_recv()
        entry_on(v).start()
        for n in range(3):
            share_out(0, v, n).start()

    def gather(v):
        for n in range(3):
            share_in(0, v, n).wait_recv()

    def gather_on(v):
        for n in range(3):
            share_in(0, v, n).wait_recv()
            direct(v, n).start()

    def second_enter(v):
        entry_in(1, v).wait_recv()
        for n in range(3):
            share_out(1, v, n).start()

    def second_gather(v):
        for n in range(3):
            share_in(1, v, n).wait_recv()
            direct(v, n).wait_recv()

    def own(i):
        if i == 4:
            swap_theta.wait_recv()
        base = core if i < 4 else 1 - core
        own_step(base * WALKERS_DEV + i % 4)

    def all_here(v):
        far_step(0, v, 0, 2 * WALKERS_DEV)

    def near_here(v):
        far_step(0, v, near_base, WALKERS_DEV)

    def next_here(v):
        far_step(1, v, next_base, WALKERS_DEV)

    @pl.when(core == 0)
    def _():
        @pl.when(y_hi == 0)
        def _():
            for v in range(VECS):
                transit_copy(v).start()

        swap_theta.start()
        swap_meta.start()
        steps = {"t": pass_on, "e": enter, "s": gather, "o": own, "a": all_here}
        for step in PLAN_0:
            steps[step[0]](int(step[1:]))

    @pl.when(core == 1)
    def _():
        for v in range(VECS):
            entry_out(slab.at[v, quarter(cross_color)], v).start()
        swap_theta.start()
        swap_meta.start()
        steps = {"e": enter_on, "s": gather_on, "f": second_enter, "g": second_gather, "o": own, "p": near_here, "q": next_here}
        for step in PLAN_1:
            steps[step[0]](int(step[1:]))

    lower = row < 4
    tile = jnp.zeros((8, LANES), jnp.float32)
    own_cols = jnp.where(lower, 4 + 4 * core, 4 * core)
    far_cols = jnp.where(lower, 12 - 12 * core, 8 + 4 * core)
    for slot in range(2 * VECS):
        cols = own_cols if slot < VECS else far_cols
        total = jnp.sum(trace[slot], axis=1, keepdims=True)
        tile = jnp.where(lane == cols + slot % VECS, total, tile)
    exch_rows = jnp.sum(exch[...], axis=1)
    tile = jnp.where(lane == EXCH_LANE, jnp.sum(exch_rows, axis=1, keepdims=True), tile)
    bias[...] = tile
    swap_bias = remote(bias, bias_in, bias_sem.at[0], bias_sem.at[1], sibling)
    swap_bias.start()
    swap_meta.wait_recv()
    known = meta[...] + meta_in[...]
    swap_bias.wait_recv()
    full = bias[...] + bias_in[...]
    is_bias = lane < STOPS * VECS

    def pick(keep, values):
        return jnp.sum(jnp.where(keep, values, 0.0), axis=1, keepdims=True)

    squares = pick(is_bias, full * full)
    drift = pick(is_bias, full * known)
    exchange = pick(lane == EXCH_LANE, full)
    energy = ONE_BODY + (0.5 * squares - 0.5 * exchange) / (NOCC * STOPS * VECS)
    weight = pick(lane == WEIGHT_LANE, known) * pick(lane == LIVE_LANE, known)
    weight = weight * jnp.exp(FIELD_COUPLING * drift - DRIFT_COST * squares)
    here = jnp.where(lane == 0, weight, jnp.where(lane == 1, weight * energy, 0.0))

    my_plane = x * 4 + y
    plane[my_plane] = here
    for d in range(1, 16):
        remote(plane.at[my_plane], plane.at[my_plane], plane_sem.at[0], plane_sem.at[1], plane_peer(d)).start()
    some = plane.at[pl.ds(0, 15)]
    remote(some, some, plane_sem.at[0], plane_sem.at[1], sibling).wait_recv()
    summed = plane[0]
    for n in range(1, 16):
        summed = summed + plane[n]
    line[z] = summed
    for d in range(1, 8):
        remote(line.at[z], line.at[z], line_sem.at[0], line_sem.at[1], line_peer(d)).start()

    table = jnp.zeros((8, LANES), jnp.float32)
    for n in range(8):
        column = plane[(n // 2) * 4 + y_hi * 2 + n % 2]
        table = jnp.where(lane == n, pick(lane == 0, column), table)
    mate = jnp.zeros((8, LANES), jnp.float32)
    for i in range(WALKERS_DEV):
        found = (row == core * 4 + (partner[i] & 3)) & (lane == partner[i] // (WALKERS_DEV * 32))
        value = jnp.sum(pick(found, table), axis=0, keepdims=True)
        mate = jnp.where(row % 4 == i, value, mate)
    paired = 0.5 * (weight + mate)

    some_line = line.at[pl.ds(0, 7)]
    remote(some_line, some_line, line_sem.at[0], line_sem.at[1], sibling).wait_recv()
    summed = line[0]
    for n in range(1, 8):
        summed = summed + line[n]
    totals = jnp.sum(summed, axis=0, keepdims=True)
    top = jnp.broadcast_to(totals, (8, LANES))
    mean = pick(lane == 1, top) / pick(lane == 0, top)
    result = jnp.where(is_bias, full, 0.0)
    result = jnp.where(lane == 16, paired, result)
    result = jnp.where(lane == 17, energy, result)
    result = jnp.where(lane == 18, mean, result)
    out[...] = jnp.where(core == 0, result[0:4], result[4:8])

    remote(some, some, plane_sem.at[0], plane_sem.at[1], sibling).wait_send()
    remote(some_line, some_line, line_sem.at[0], line_sem.at[1], sibling).wait_send()
    swap_bias.wait_send()
    swap_theta.wait_send()
    swap_meta.wait_send()

    def sent(v, carry):
        for n in range(3):
            share_out(0, v, n).wait_send()

        @pl.when(core == 0)
        def _():
            @pl.when(y_hi == 0)
            def _():
                transit_copy(v).wait_send()

        entry_out(transit.at[v], v).wait_send()

        @pl.when(core == 1)
        def _():
            entry_on(v).wait_send()
            for n in range(3):
                share_out(1, v, n).wait_send()
                direct(v, n).wait_send()

        return carry

    lax.fori_loop(0, VECS, sent, 0)


def body(chol, green, fields, weights_in, partner, counts):
    anywhere = pl.BlockSpec(memory_space=pl.ANY)
    vmem = pl.BlockSpec(memory_space=pltpu.VMEM)
    dma = pltpu.SemaphoreType.DMA
    tile = pltpu.VMEM((8, LANES), jnp.float32)
    out = pl.pallas_call(
        kernel,
        out_shape=jax.ShapeDtypeStruct((4, LANES), jnp.float32),
        in_specs=[anywhere] * 6,
        out_specs=vmem,
        scratch_shapes=[
            pltpu.VMEM((WALKERS_DEV, STOPS * VECS), jnp.float32),
            pltpu.SMEM((WALKERS_DEV,), jnp.float32),
            pltpu.SMEM((WALKERS_DEV,), jnp.int32),
            pltpu.SMEM((1, 1), jnp.int32),
            pltpu.VMEM((VECS, NOCC, ORB), jnp.bfloat16),
            pltpu.VMEM((2 * WALKERS_DEV, ORB, NOCC), jnp.bfloat16),
            pltpu.VMEM((2, VECS, NOCC, ORB), jnp.bfloat16),
            pltpu.VMEM((VECS, QUARTER, ORB), jnp.bfloat16),
            pltpu.VMEM((2 * VECS, 8, LANES), jnp.float32),
            pltpu.VMEM((8, 8, LANES), jnp.float32),
            tile, tile, tile, tile,
            pltpu.VMEM((16, 8, LANES), jnp.float32),
            pltpu.VMEM((8, 8, LANES), jnp.float32),
            dma((4,)), dma((2,)), dma((2,)), dma((2,)), dma((2,)),
            dma((2, VECS)), dma((2, VECS)), dma((VECS,)), dma((VECS,)),
            dma((2, VECS, 3)), dma((2, VECS, 3)), dma((VECS, 3)), dma((VECS, 3)),
            dma((2,)), dma((2,)),
        ],
        compiler_params=pltpu.CompilerParams(
            collective_id=0, has_side_effects=True, vmem_limit_bytes=62 * 2**20
        ),
        name="walkers",
    )(chol, green, fields, weights_in, partner, counts)
    return out[:, 16], out[:, 17], out[:, : STOPS * VECS], out[0, 18]


def solution(mesh):
    placed = (
        P("ham", None, None),
        P(("walk", "ham"), None, None),
        P(("walk", "ham"), None),
        P(("walk", "ham")),
        P(("walk", "ham")),
        P("walk", "ham"),
    )
    return jax.shard_map(
        body,
        mesh=mesh,
        in_specs=placed,
        out_specs=(P(("walk", "ham")), P(("walk", "ham")), P(("walk", "ham"), None), P()),
        check_vma=False,
    )
```

```python
import functools

import jax
import jax.numpy as jnp
from jax import lax
from jax.experimental import pallas as pl
from jax.experimental.pallas import tpu as pltpu
from jax.sharding import PartitionSpec as P

ORB = 1024
NOCC = 256
VECS = 4
STOPS = 4
WALKERS_DEV = 4
QUARTER = NOCC // 4
EIGHTH = NOCC // 8
FIELD_COUPLING = 0.02
DRIFT_COST = 0.0002
ONE_BODY = 1.0
MESH = pl.DeviceIdType.MESH
LANES = 128
EXCH_LANE = 16
WEIGHT_LANE = 17
LIVE_LANE = 18
PLAN_0 = (
    "o0", "o1", "t0", "o2", "t1", "o3", "t2", "w0", "m0", "t3", "e0", "m1",
    "e1", "m2", "e2", "s0", "a0", "e3", "b0", "s1", "a1", "b1", "m3", "s2",
    "a2", "b2", "s3", "a3", "b3",
)
PLAN_1 = (
    "o0", "o1", "o2", "o3", "e0", "w0", "m0", "e1", "m1", "e2", "f0", "s0",
    "m2", "e3", "f1", "s1", "p0", "f2", "s2", "p1", "m3", "f3", "s3", "p2",
    "g0", "q0", "p3", "g1", "q1", "g2", "q2", "g3", "q3",
)


def rounds_of(plan, kinds):
    rounds, steps = [], {}
    order = list(kinds)
    for name in plan:
        kind = name[0]
        if kind in kinds:
            assert kind not in steps and all(order.index(k) < order.index(kind) for k in steps), name
            steps[kind] = int(name[1:])
        else:
            rounds.append((steps, name))
            steps = {}
    assert not steps
    return rounds


def product_terms(prod):
    a, b = prod[:128, :128], prod[:128, 128:]
    c, d = prod[128:, :128], prod[128:, 128:]
    i = lax.broadcasted_iota(jnp.int32, (128, 128), 0)
    j = lax.broadcasted_iota(jnp.int32, (128, 128), 1)
    low = jnp.where(i >= j, a, d)
    high = jnp.where(i < j, a, d)
    pairs = high * low.T + b * c.T
    gap = jnp.where(i == j, a - d, 0.0)
    diag = jnp.where(i == j, a + d, 0.0)
    exchange = jnp.sum((pairs + pairs + gap * gap).reshape(16, 8, 128), axis=0)
    trace = jnp.sum(diag, axis=0, keepdims=True)
    return trace, exchange


def kernel(
    chol, green, fields_in, weights_in, partner_in, counts_in, out,
    fields, weights, partner, counts, vecs, theta, carry, transit, trace, exch, meta, meta_in, bias, bias_in, plane, line,
    small_sem, load_sem, theta_sem, meta_sem, bias_sem, entry_send, entry_recv, transit_send, transit_recv,
    share_send, share_recv, direct_send, direct_recv, plane_sem, line_sem,
):
    h, g = lax.axis_index("ham"), lax.axis_index("walk")
    z, y_hi, core = h // 4, lax.rem(h // 2, 2), lax.rem(h, 2)
    x, y_lo = g // 2, lax.rem(g, 2)
    y = y_hi * 2 + y_lo

    def device(x=x, y_hi=y_hi, y_lo=y_lo, z=z, core=core):
        return {"ham": z * 4 + y_hi * 2 + core, "walk": x * 2 + y_lo}

    sibling = device(core=1 - core)
    cross = device(y_hi=1 - y_hi, y_lo=1 - y_lo)
    twin = device(y_lo=1 - y_lo)
    x_up, x_down = device(x=lax.rem(x + 1, 4)), device(x=lax.rem(x + 3, 4))
    z_down = device(z=lax.rem(z + 7, 8))
    z_on = device(z=lax.rem(z + 9 - 2 * y_hi, 8))
    sharers = (x_down, x_up, twin)
    color = lax.rem(x + 2 * y_lo, 4)
    cross_color = lax.rem(x + 2 * (1 - y_lo), 4)
    colors = (lax.rem(color + 1, 4), lax.rem(color + 3, 4), lax.rem(color + 2, 4))

    def plane_peer(d):
        yy = lax.rem(y + d // 4, 4)
        return device(x=lax.rem(x + d % 4, 4), y_hi=yy // 2, y_lo=lax.rem(yy, 2))

    def line_peer(d):
        return device(z=lax.rem(z + d, 8))

    def quarter(k):
        return pl.ds(pl.multiple_of(k * QUARTER, QUARTER), QUARTER)

    def first(k):
        return pl.ds(pl.multiple_of(k * QUARTER, EIGHTH), EIGHTH)

    def second(k):
        return pl.ds(pl.multiple_of(k * QUARTER + EIGHTH, EIGHTH), EIGHTH)

    def remote(src, dst, send, recv, to):
        return pltpu.make_async_remote_copy(src, dst, send, recv, device_id=to, device_id_type=MESH)

    own_rows = pl.ds(core * WALKERS_DEV, WALKERS_DEV)
    small = [
        pltpu.make_async_copy(src, dst, small_sem.at[n])
        for n, (src, dst) in enumerate(
            ((fields_in, fields), (weights_in, weights), (partner_in, partner), (counts_in, counts))
        )
    ]
    for copy in small:
        copy.start()
    load_slab = pltpu.make_async_copy(chol, vecs.at[0], load_sem.at[0])
    load_theta = pltpu.make_async_copy(green, theta.at[own_rows], load_sem.at[1])
    load_slab.start()
    load_theta.start()

    barrier = pltpu.get_barrier_semaphore()
    pl.semaphore_signal(barrier, inc=1, device_id=sibling, device_id_type=MESH)
    for d in range(1, 16):
        pl.semaphore_signal(barrier, inc=1, device_id=plane_peer(d), device_id_type=MESH)
    for d in range(1, 8):
        pl.semaphore_signal(barrier, inc=1, device_id=line_peer(d), device_id_type=MESH)

    for copy in small:
        copy.wait()
    row = lax.broadcasted_iota(jnp.int32, (8, LANES), 0)
    lane = lax.broadcasted_iota(jnp.int32, (8, LANES), 1)
    mine = row // 4 == core
    meta[...] = jnp.zeros_like(meta)
    meta[0:4, 0:16] = fields[...]
    meta[4:8, 0:16] = fields[...]
    values = meta[...]
    for i in range(WALKERS_DEV):
        values = jnp.where((row % 4 == i) & (lane == WEIGHT_LANE), weights[i], values)
    values = jnp.where((row % 4 < counts[0, 0]) & (lane == LIVE_LANE), 1.0, values)
    meta[...] = jnp.where(mine, values, 0.0)
    exch[...] = jnp.zeros_like(exch)

    load_slab.wait()
    load_theta.wait()
    pl.semaphore_wait(barrier, 23)

    swap_theta = remote(theta.at[own_rows], theta.at[own_rows], theta_sem.at[0], theta_sem.at[1], sibling)
    swap_meta = remote(meta, meta_in, meta_sem.at[0], meta_sem.at[1], sibling)

    def entry_out(src, v):
        return remote(src, vecs.at[1, v, quarter(cross_color)], entry_send.at[0, v], entry_recv.at[0, v], cross)

    def entry_in(s, v):
        rows = vecs.at[1 + s, v, quarter(color)]
        return remote(rows, rows, entry_send.at[s, v], entry_recv.at[s, v], cross)

    def entry_on(v):
        rows = vecs.at[1, v, quarter(color)]
        return remote(rows, vecs.at[2, v, quarter(color)], entry_send.at[1, v], entry_recv.at[1, v], z_on)

    def transit_copy(v):
        return remote(vecs.at[0, v, quarter(cross_color)], transit.at[v], transit_send.at[v], transit_recv.at[v], z_down)

    def part(s, k):
        return quarter(k) if s == 0 else first(k)

    def share_out(s, v, n):
        rows = vecs.at[1 + s, v, part(s, color)]
        return remote(rows, rows, share_send.at[s, v, n], share_recv.at[s, v, n], sharers[n])

    def share_in(s, v, n):
        rows = vecs.at[1 + s, v, part(s, colors[n])]
        return remote(rows, rows, share_send.at[s, v, n], share_recv.at[s, v, n], sharers[n])

    def direct(v, n):
        rows = second(colors[n])
        return remote(vecs.at[1, v, rows], vecs.at[2, v, rows], direct_send.at[v, n], direct_recv.at[v, n], z_on)

    def note(slot, w, prod):
        diagonal, exchange = product_terms(prod)
        trace[slot, pl.ds(w, 1), :] = diagonal
        exch[w] += exchange

    def unit(s, v, base, last_slot, last_w):
        slot = jnp.where(s == 0, v, VECS + v)
        vector = vecs[s, v]
        note(last_slot, last_w, carry[...])
        for n in range(WALKERS_DEV):
            prod = jnp.dot(vector, theta[base + n], preferred_element_type=jnp.float32)
            if n < WALKERS_DEV - 1:
                note(slot, base + n, prod)
            else:
                carry[...] = prod
        return slot, base + WALKERS_DEV - 1

    mine_base, other_base = core * WALKERS_DEV, (1 - core) * WALKERS_DEV
    near_base = (1 - y_hi) * WALKERS_DEV
    next_base = y_hi * WALKERS_DEV

    def pass_on(v):
        @pl.when(y_hi == 0)
        def _():
            transit_copy(v).wait_recv()
            entry_out(transit.at[v], v).start()

        @pl.when(y_hi == 1)
        def _():
            entry_out(vecs.at[0, v, quarter(cross_color)], v).start()

    def enter(v):
        entry_in(0, v).wait_recv()
        for n in range(3):
            share_out(0, v, n).start()

    def enter_on(v):
        entry_in(0, v).wait_recv()
        entry_on(v).start()
        for n in range(3):
            share_out(0, v, n).start()

    def gather(v):
        for n in range(3):
            share_in(0, v, n).wait_recv()

    def gather_on(v):
        for n in range(3):
            share_in(0, v, n).wait_recv()
            direct(v, n).start()

    def second_enter(v):
        entry_in(1, v).wait_recv()
        for n in range(3):
            share_out(1, v, n).start()

    def second_gather(v):
        for n in range(3):
            share_in(1, v, n).wait_recv()
            direct(v, n).wait_recv()

    def swapped(v):
        swap_theta.wait_recv()

    def run(plan, steps, units):
        rounds = rounds_of(plan, steps)

        def round_(i, last):
            for kind, action in steps.items():
                at = [(n, r[0][kind]) for n, r in enumerate(rounds) if kind in r[0]]
                if at:
                    v = sum(jnp.where(i == n, step, 0) for n, step in at)
                    hit = functools.reduce(jnp.logical_or, [i == n for n, _ in at])
                    pl.when(hit)(functools.partial(action, v))

            def pick(field):
                return sum(jnp.where(i == n, units(r[1])[field], 0) for n, r in enumerate(rounds))

            return unit(pick(0), pick(1), pick(2), *last)

        slot, w = lax.fori_loop(0, len(rounds), round_, (jnp.int32(0), jnp.int32(0)))
        note(slot, w, carry[...])

    own_units = {"o": (0, mine_base), "m": (0, other_base)}

    def unit_of(table):
        return lambda name: (table[name[0]][0], int(name[1:]), table[name[0]][1])

    carry[...] = jnp.zeros_like(carry)

    @pl.when(core == 0)
    def _():
        @pl.when(y_hi == 0)
        def _():
            for v in range(VECS):
                transit_copy(v).start()

        swap_theta.start()
        swap_meta.start()
        steps = {"t": pass_on, "e": enter, "s": gather, "w": swapped}
        run(PLAN_0, steps, unit_of(own_units | {"a": (1, mine_base), "b": (1, other_base)}))

    @pl.when(core == 1)
    def _():
        for v in range(VECS):
            entry_out(vecs.at[0, v, quarter(cross_color)], v).start()
        swap_theta.start()
        swap_meta.start()
        steps = {"e": enter_on, "f": second_enter, "s": gather_on, "g": second_gather, "w": swapped}
        run(PLAN_1, steps, unit_of(own_units | {"p": (1, near_base), "q": (2, next_base)}))

    lower = row < 4
    tile = jnp.zeros((8, LANES), jnp.float32)
    own_cols = jnp.where(lower, 4 + 4 * core, 4 * core)
    far_cols = jnp.where(lower, 12 - 12 * core, 8 + 4 * core)
    for slot in range(2 * VECS):
        cols = own_cols if slot < VECS else far_cols
        total = jnp.sum(trace[slot], axis=1, keepdims=True)
        tile = jnp.where(lane == cols + slot % VECS, total, tile)
    exch_rows = jnp.sum(exch[...], axis=1)
    tile = jnp.where(lane == EXCH_LANE, jnp.sum(exch_rows, axis=1, keepdims=True), tile)
    bias[...] = tile
    swap_bias = remote(bias, bias_in, bias_sem.at[0], bias_sem.at[1], sibling)
    swap_bias.start()
    swap_meta.wait_recv()
    known = meta[...] + meta_in[...]
    swap_bias.wait_recv()
    full = bias[...] + bias_in[...]
    is_bias = lane < STOPS * VECS

    def pick(keep, values):
        return jnp.sum(jnp.where(keep, values, 0.0), axis=1, keepdims=True)

    squares = pick(is_bias, full * full)
    drift = pick(is_bias, full * known)
    exchange = pick(lane == EXCH_LANE, full)
    energy = ONE_BODY + (0.5 * squares - 0.5 * exchange) / (NOCC * STOPS * VECS)
    weight = pick(lane == WEIGHT_LANE, known) * pick(lane == LIVE_LANE, known)
    weight = weight * jnp.exp(FIELD_COUPLING * drift - DRIFT_COST * squares)
    here = jnp.where(lane == 0, weight, jnp.where(lane == 1, weight * energy, 0.0))

    my_plane = x * 4 + y
    plane[my_plane] = here
    for d in range(1, 16):
        remote(plane.at[my_plane], plane.at[my_plane], plane_sem.at[0], plane_sem.at[1], plane_peer(d)).start()
    some = plane.at[pl.ds(0, 15)]
    remote(some, some, plane_sem.at[0], plane_sem.at[1], sibling).wait_recv()
    summed = plane[0]
    for n in range(1, 16):
        summed = summed + plane[n]
    line[z] = summed
    for d in range(1, 8):
        remote(line.at[z], line.at[z], line_sem.at[0], line_sem.at[1], line_peer(d)).start()

    table = jnp.zeros((8, LANES), jnp.float32)
    for n in range(8):
        column = plane[(n // 2) * 4 + y_hi * 2 + n % 2]
        table = jnp.where(lane == n, pick(lane == 0, column), table)
    mate = jnp.zeros((8, LANES), jnp.float32)
    for i in range(WALKERS_DEV):
        found = (row == core * 4 + (partner[i] & 3)) & (lane == partner[i] // (WALKERS_DEV * 32))
        value = jnp.sum(pick(found, table), axis=0, keepdims=True)
        mate = jnp.where(row % 4 == i, value, mate)
    paired = 0.5 * (weight + mate)

    some_line = line.at[pl.ds(0, 7)]
    remote(some_line, some_line, line_sem.at[0], line_sem.at[1], sibling).wait_recv()
    summed = line[0]
    for n in range(1, 8):
        summed = summed + line[n]
    totals = jnp.sum(summed, axis=0, keepdims=True)
    top = jnp.broadcast_to(totals, (8, LANES))
    mean = pick(lane == 1, top) / pick(lane == 0, top)
    result = jnp.where(is_bias, full, 0.0)
    result = jnp.where(lane == 16, paired, result)
    result = jnp.where(lane == 17, energy, result)
    result = jnp.where(lane == 18, mean, result)
    out[...] = jnp.where(core == 0, result[0:4], result[4:8])

    remote(some, some, plane_sem.at[0], plane_sem.at[1], sibling).wait_send()
    remote(some_line, some_line, line_sem.at[0], line_sem.at[1], sibling).wait_send()
    swap_bias.wait_send()
    swap_theta.wait_send()
    swap_meta.wait_send()

    def sent(v, carry):
        for n in range(3):
            share_out(0, v, n).wait_send()

        @pl.when(core == 0)
        def _():
            @pl.when(y_hi == 0)
            def _():
                transit_copy(v).wait_send()

        entry_out(transit.at[v], v).wait_send()

        @pl.when(core == 1)
        def _():
            entry_on(v).wait_send()
            for n in range(3):
                share_out(1, v, n).wait_send()
                direct(v, n).wait_send()

        return carry

    lax.fori_loop(0, VECS, sent, 0)


def body(chol, green, fields, weights_in, partner, counts):
    anywhere = pl.BlockSpec(memory_space=pl.ANY)
    vmem = pl.BlockSpec(memory_space=pltpu.VMEM)
    dma = pltpu.SemaphoreType.DMA
    tile = pltpu.VMEM((8, LANES), jnp.float32)
    out = pl.pallas_call(
        kernel,
        out_shape=jax.ShapeDtypeStruct((4, LANES), jnp.float32),
        in_specs=[anywhere] * 6,
        out_specs=vmem,
        scratch_shapes=[
            pltpu.VMEM((WALKERS_DEV, STOPS * VECS), jnp.float32),
            pltpu.SMEM((WALKERS_DEV,), jnp.float32),
            pltpu.SMEM((WALKERS_DEV,), jnp.int32),
            pltpu.SMEM((1, 1), jnp.int32),
            pltpu.VMEM((3, VECS, NOCC, ORB), jnp.bfloat16),
            pltpu.VMEM((2 * WALKERS_DEV, ORB, NOCC), jnp.bfloat16),
            pltpu.VMEM((NOCC, NOCC), jnp.float32),
            pltpu.VMEM((VECS, QUARTER, ORB), jnp.bfloat16),
            pltpu.VMEM((2 * VECS, 8, LANES), jnp.float32),
            pltpu.VMEM((8, 8, LANES), jnp.float32),
            tile, tile, tile, tile,
            pltpu.VMEM((16, 8, LANES), jnp.float32),
            pltpu.VMEM((8, 8, LANES), jnp.float32),
            dma((4,)), dma((2,)), dma((2,)), dma((2,)), dma((2,)),
            dma((2, VECS)), dma((2, VECS)), dma((VECS,)), dma((VECS,)),
            dma((2, VECS, 3)), dma((2, VECS, 3)), dma((VECS, 3)), dma((VECS, 3)),
            dma((2,)), dma((2,)),
        ],
        compiler_params=pltpu.CompilerParams(
            collective_id=0, has_side_effects=True, vmem_limit_bytes=62 * 2**20
        ),
        name="walkers",
    )(chol, green, fields, weights_in, partner, counts)
    return out[:, 16], out[:, 17], out[:, : STOPS * VECS], out[0, 18]


def solution(mesh):
    placed = (
        P("ham", None, None),
        P(("walk", "ham"), None, None),
        P(("walk", "ham"), None),
        P(("walk", "ham")),
        P(("walk", "ham")),
        P("walk", "ham"),
    )
    return jax.shard_map(
        body,
        mesh=mesh,
        in_specs=placed,
        out_specs=(P(("walk", "ham")), P(("walk", "ham")), P(("walk", "ham"), None), P()),
        check_vma=False,
    )
```

```python
import functools

import jax
import jax.numpy as jnp
from jax import lax
from jax.experimental import pallas as pl
from jax.experimental.pallas import tpu as pltpu
from jax.sharding import PartitionSpec as P

ORB = 1024
NOCC = 256
VECS = 4
STOPS = 4
WALKERS_DEV = 4
QUARTER = NOCC // 4
EIGHTH = NOCC // 8
FIELD_COUPLING = 0.02
DRIFT_COST = 0.0002
ONE_BODY = 1.0
MESH = pl.DeviceIdType.MESH
LANES = 128
EXCH_LANE = 16
WEIGHT_LANE = 17
LIVE_LANE = 18
PLAN_0 = (
    "o0", "t0", "o1", "t1", "e0", "o2", "t2", "o3", "t3", "e1", "w0", "m0",
    "m1", "m2", "e2", "m3", "s0", "a0", "e3", "b0", "s1", "a1", "b1", "s2",
    "b2", "a2", "s3", "b3", "a3",
)
PLAN_1 = (
    "o0", "e0", "o1", "e1", "o2", "e2", "f0", "s0", "o3", "e3", "f1", "s1",
    "w0", "p0", "m0", "p1", "f2", "s2", "p2", "g0", "q0", "m1", "s3", "p3",
    "f3", "g1", "m2", "m3", "q1", "g2", "q2", "g3", "q3",
)


def rounds_of(plan, kinds):
    rounds, steps = [], {}
    order = list(kinds)
    for name in plan:
        kind = name[0]
        if kind in kinds:
            assert kind not in steps and all(order.index(k) < order.index(kind) for k in steps), name
            steps[kind] = int(name[1:])
        else:
            rounds.append((steps, name))
            steps = {}
    assert not steps
    return rounds


def product_terms(prod):
    a, b = prod[:128, :128], prod[:128, 128:]
    c, d = prod[128:, :128], prod[128:, 128:]
    i = lax.broadcasted_iota(jnp.int32, (128, 128), 0)
    j = lax.broadcasted_iota(jnp.int32, (128, 128), 1)
    low = jnp.where(i >= j, a, d)
    high = jnp.where(i < j, a, d)
    pairs = high * low.T + b * c.T
    gap = jnp.where(i == j, a - d, 0.0)
    diag = jnp.where(i == j, a + d, 0.0)
    exchange = jnp.sum((pairs + pairs + gap * gap).reshape(16, 8, 128), axis=0)
    trace = jnp.sum(diag, axis=0, keepdims=True)
    return trace, exchange


def kernel(
    chol, green, fields_in, weights_in, partner_in, counts, out,
    fields, weights, partner, vecs, theta, carry, transit, trace, exch, meta, meta_in, bias, bias_in, plane, line,
    small_sem, load_sem, theta_sem, meta_sem, bias_sem, entry_send, entry_recv, transit_send, transit_recv,
    share_send, share_recv, direct_send, direct_recv, plane_sem, line_sem, hail_sem,
):
    h, g = lax.axis_index("ham"), lax.axis_index("walk")
    z, y_hi, core = h // 4, lax.rem(h // 2, 2), lax.rem(h, 2)
    x, y_lo = g // 2, lax.rem(g, 2)
    y = y_hi * 2 + y_lo

    def device(x=x, y_hi=y_hi, y_lo=y_lo, z=z, core=core):
        return {"ham": z * 4 + y_hi * 2 + core, "walk": x * 2 + y_lo}

    sibling = device(core=1 - core)
    cross = device(y_hi=1 - y_hi, y_lo=1 - y_lo)
    twin = device(y_lo=1 - y_lo)
    x_up, x_down = device(x=lax.rem(x + 1, 4)), device(x=lax.rem(x + 3, 4))
    z_down = device(z=lax.rem(z + 7, 8))
    z_on = device(z=lax.rem(z + 9 - 2 * y_hi, 8))
    sharers = (x_down, x_up, twin)
    color = lax.rem(x + 2 * y_lo, 4)
    cross_color = lax.rem(x + 2 * (1 - y_lo), 4)
    colors = (lax.rem(color + 1, 4), lax.rem(color + 3, 4), lax.rem(color + 2, 4))

    def plane_peer(d):
        yy = lax.rem(y + d // 4, 4)
        return device(x=lax.rem(x + d % 4, 4), y_hi=yy // 2, y_lo=lax.rem(yy, 2))

    def line_peer(d):
        return device(z=lax.rem(z + d, 8))

    def quarter(k):
        return pl.ds(pl.multiple_of(k * QUARTER, QUARTER), QUARTER)

    def first(k):
        return pl.ds(pl.multiple_of(k * QUARTER, EIGHTH), EIGHTH)

    def second(k):
        return pl.ds(pl.multiple_of(k * QUARTER + EIGHTH, EIGHTH), EIGHTH)

    def remote(src, dst, send, recv, to):
        return pltpu.make_async_remote_copy(src, dst, send, recv, device_id=to, device_id_type=MESH)

    own_rows = pl.ds(core * WALKERS_DEV, WALKERS_DEV)
    small = [
        pltpu.make_async_copy(src, dst, small_sem.at[n])
        for n, (src, dst) in enumerate(
            ((fields_in, fields), (weights_in, weights), (partner_in, partner))
        )
    ]
    for copy in small:
        copy.start()
    load_slab = pltpu.make_async_copy(chol, vecs.at[0], load_sem.at[0])
    load_theta = pltpu.make_async_copy(green, theta.at[own_rows], load_sem.at[1])
    load_slab.start()
    load_theta.start()

    def hail(n):
        for peer in neighbours:
            pl.semaphore_signal(hail_sem.at[n], inc=1, device_id=peer, device_id_type=MESH)

    def heard(n):
        pl.semaphore_wait(hail_sem.at[n], 6)
        if n < 2:
            hail(n + 1)

    barrier = pltpu.get_barrier_semaphore()
    neighbours = (x_up, x_down, cross, twin, line_peer(1), line_peer(7))
    for peer in (sibling, *neighbours):
        pl.semaphore_signal(barrier, inc=1, device_id=peer, device_id_type=MESH)

    for copy in small:
        copy.wait()
    row = lax.broadcasted_iota(jnp.int32, (8, LANES), 0)
    lane = lax.broadcasted_iota(jnp.int32, (8, LANES), 1)
    mine = row // 4 == core
    meta[...] = jnp.zeros_like(meta)
    meta[0:4, 0:16] = fields[...]
    meta[4:8, 0:16] = fields[...]
    values = meta[...]
    for i in range(WALKERS_DEV):
        values = jnp.where((row % 4 == i) & (lane == WEIGHT_LANE), weights[i], values)
    values = jnp.where((row % 4 < counts[0, 0]) & (lane == LIVE_LANE), 1.0, values)
    meta[...] = jnp.where(mine, values, 0.0)
    exch[...] = jnp.zeros_like(exch)

    pl.semaphore_wait(barrier, 7)

    swap_theta = remote(green, theta.at[own_rows], theta_sem.at[0], theta_sem.at[1], sibling)
    swap_meta = remote(meta, meta_in, meta_sem.at[0], meta_sem.at[1], sibling)

    def entry_out(src, v):
        return remote(src, vecs.at[1, v, quarter(cross_color)], entry_send.at[0, v], entry_recv.at[0, v], cross)

    def entry_in(s, v):
        rows = vecs.at[1 + s, v, quarter(color)]
        return remote(rows, rows, entry_send.at[s, v], entry_recv.at[s, v], cross)

    def entry_on(v):
        rows = vecs.at[1, v, quarter(color)]
        return remote(rows, vecs.at[2, v, quarter(color)], entry_send.at[1, v], entry_recv.at[1, v], z_on)

    def transit_copy(v):
        return remote(chol.at[v, quarter(cross_color)], transit.at[v], transit_send.at[v], transit_recv.at[v], z_down)

    def part(s, k):
        return quarter(k) if s == 0 else first(k)

    def share_out(s, v, n):
        rows = vecs.at[1 + s, v, part(s, color)]
        return remote(rows, rows, share_send.at[s, v, n], share_recv.at[s, v, n], sharers[n])

    def share_in(s, v, n):
        rows = vecs.at[1 + s, v, part(s, colors[n])]
        return remote(rows, rows, share_send.at[s, v, n], share_recv.at[s, v, n], sharers[n])

    def direct(v, n):
        rows = second(colors[n])
        return remote(vecs.at[1, v, rows], vecs.at[2, v, rows], direct_send.at[v, n], direct_recv.at[v, n], z_on)

    def note(slot, w, prod):
        diagonal, exchange = product_terms(prod)
        trace[slot, pl.ds(w, 1), :] = diagonal
        exch[w] += exchange

    def unit(s, v, base, last_slot, last_w):
        slot = jnp.where(s == 0, v, VECS + v)
        vector = vecs[s, v]
        note(last_slot, last_w, carry[...])
        for n in range(WALKERS_DEV):
            prod = jnp.dot(vector, theta[base + n], preferred_element_type=jnp.float32)
            if n < WALKERS_DEV - 1:
                note(slot, base + n, prod)
            else:
                carry[...] = prod
        return slot, base + WALKERS_DEV - 1

    mine_base, other_base = core * WALKERS_DEV, (1 - core) * WALKERS_DEV
    near_base = (1 - y_hi) * WALKERS_DEV
    next_base = y_hi * WALKERS_DEV

    def pass_on(v):
        @pl.when(y_hi == 0)
        def _():
            transit_copy(v).wait_recv()
            entry_out(transit.at[v], v).start()

        @pl.when(y_hi == 1)
        def _():
            entry_out(chol.at[v, quarter(cross_color)], v).start()

    def enter(v):
        entry_in(0, v).wait_recv()
        for n in range(3):
            share_out(0, v, n).start()

    def enter_on(v):
        entry_in(0, v).wait_recv()
        entry_on(v).start()
        for n in range(3):
            share_out(0, v, n).start()

    def gather(v):
        for n in range(3):
            share_in(0, v, n).wait_recv()

    def gather_on(v):
        for n in range(3):
            share_in(0, v, n).wait_recv()
            direct(v, n).start()

    def second_enter(v):
        entry_in(1, v).wait_recv()
        for n in range(3):
            share_out(1, v, n).start()

    def second_gather(v):
        for n in range(3):
            share_in(1, v, n).wait_recv()
            direct(v, n).wait_recv()

    def swapped(v):
        swap_theta.wait_recv()

    def run(plan, steps, units):
        rounds = rounds_of(plan, steps)

        def round_(i, last):
            for n in range(3):
                pl.when(i == 3 * n + 2)(functools.partial(heard, n))

            for kind, action in steps.items():
                at = [(n, r[0][kind]) for n, r in enumerate(rounds) if kind in r[0]]
                if at:
                    v = sum(jnp.where(i == n, step, 0) for n, step in at)
                    hit = functools.reduce(jnp.logical_or, [i == n for n, _ in at])
                    pl.when(hit)(functools.partial(action, v))

            def pick(field):
                return sum(jnp.where(i == n, units(r[1])[field], 0) for n, r in enumerate(rounds))

            return unit(pick(0), pick(1), pick(2), *last)

        slot, w = lax.fori_loop(0, len(rounds), round_, (jnp.int32(0), jnp.int32(0)))
        note(slot, w, carry[...])

    own_units = {"o": (0, mine_base), "m": (0, other_base)}

    def unit_of(table):
        return lambda name: (table[name[0]][0], int(name[1:]), table[name[0]][1])

    carry[...] = jnp.zeros_like(carry)

    @pl.when(core == 0)
    def _():
        @pl.when(y_hi == 0)
        def _():
            for v in range(VECS):
                transit_copy(v).start()

        swap_theta.start()
        swap_meta.start()
        hail(0)
        load_slab.wait()
        load_theta.wait()
        steps = {"t": pass_on, "e": enter, "s": gather, "w": swapped}
        run(PLAN_0, steps, unit_of(own_units | {"a": (1, mine_base), "b": (1, other_base)}))

    @pl.when(core == 1)
    def _():
        for v in range(VECS):
            entry_out(chol.at[v, quarter(cross_color)], v).start()
        swap_theta.start()
        swap_meta.start()
        hail(0)
        load_slab.wait()
        load_theta.wait()
        steps = {"e": enter_on, "f": second_enter, "s": gather_on, "g": second_gather, "w": swapped}
        run(PLAN_1, steps, unit_of(own_units | {"p": (1, near_base), "q": (2, next_base)}))

    lower = row < 4
    tile = jnp.zeros((8, LANES), jnp.float32)
    own_cols = jnp.where(lower, 4 + 4 * core, 4 * core)
    far_cols = jnp.where(lower, 12 - 12 * core, 8 + 4 * core)
    for slot in range(2 * VECS):
        cols = own_cols if slot < VECS else far_cols
        total = jnp.sum(trace[slot], axis=1, keepdims=True)
        tile = jnp.where(lane == cols + slot % VECS, total, tile)
    exch_rows = jnp.sum(exch[...], axis=1)
    tile = jnp.where(lane == EXCH_LANE, jnp.sum(exch_rows, axis=1, keepdims=True), tile)
    bias[...] = tile
    swap_bias = remote(bias, bias_in, bias_sem.at[0], bias_sem.at[1], sibling)
    swap_bias.start()
    swap_meta.wait_recv()
    known = meta[...] + meta_in[...]
    swap_bias.wait_recv()
    full = bias[...] + bias_in[...]
    is_bias = lane < STOPS * VECS

    def pick(keep, values):
        return jnp.sum(jnp.where(keep, values, 0.0), axis=1, keepdims=True)

    squares = pick(is_bias, full * full)
    drift = pick(is_bias, full * known)
    exchange = pick(lane == EXCH_LANE, full)
    energy = ONE_BODY + (0.5 * squares - 0.5 * exchange) / (NOCC * STOPS * VECS)
    weight = pick(lane == WEIGHT_LANE, known) * pick(lane == LIVE_LANE, known)
    weight = weight * jnp.exp(FIELD_COUPLING * drift - DRIFT_COST * squares)
    here = jnp.where(lane == 0, weight, jnp.where(lane == 1, weight * energy, 0.0))

    my_plane = x * 4 + y
    plane[my_plane] = here
    for d in range(1, 16):
        remote(plane.at[my_plane], plane.at[my_plane], plane_sem.at[0], plane_sem.at[1], plane_peer(d)).start()
    some = plane.at[pl.ds(0, 15)]
    remote(some, some, plane_sem.at[0], plane_sem.at[1], sibling).wait_recv()
    summed = plane[0]
    for n in range(1, 16):
        summed = summed + plane[n]
    line[z] = summed
    for d in range(1, 8):
        remote(line.at[z], line.at[z], line_sem.at[0], line_sem.at[1], line_peer(d)).start()

    table = jnp.zeros((8, LANES), jnp.float32)
    for n in range(8):
        column = plane[(n // 2) * 4 + y_hi * 2 + n % 2]
        table = jnp.where(lane == n, pick(lane == 0, column), table)
    mate = jnp.zeros((8, LANES), jnp.float32)
    for i in range(WALKERS_DEV):
        found = (row == core * 4 + (partner[i] & 3)) & (lane == partner[i] // (WALKERS_DEV * 32))
        value = jnp.sum(pick(found, table), axis=0, keepdims=True)
        mate = jnp.where(row % 4 == i, value, mate)
    paired = 0.5 * (weight + mate)

    some_line = line.at[pl.ds(0, 7)]
    remote(some_line, some_line, line_sem.at[0], line_sem.at[1], sibling).wait_recv()
    summed = line[0]
    for n in range(1, 8):
        summed = summed + line[n]
    totals = jnp.sum(summed, axis=0, keepdims=True)
    top = jnp.broadcast_to(totals, (8, LANES))
    mean = pick(lane == 1, top) / pick(lane == 0, top)
    eye = (row == lane) | (row == lane + 4)
    keep = eye & mine

    def along(values):
        return jnp.sum(jnp.where(keep, values, 0.0), axis=0, keepdims=True)

    biases = jnp.where(core == 0, full[0:4], full[4:8])
    out[0:4, :] = jnp.where(is_bias[0:4], biases, 0.0)
    out[4:5, :] = along(paired)
    out[5:6, :] = along(energy)
    out[6:7, :] = mean[0:1] + jnp.zeros((1, LANES), jnp.float32)

    remote(some, some, plane_sem.at[0], plane_sem.at[1], sibling).wait_send()
    remote(some_line, some_line, line_sem.at[0], line_sem.at[1], sibling).wait_send()
    swap_bias.wait_send()
    swap_theta.wait_send()
    swap_meta.wait_send()

    def sent(v, carry):
        for n in range(3):
            share_out(0, v, n).wait_send()

        @pl.when(core == 0)
        def _():
            @pl.when(y_hi == 0)
            def _():
                transit_copy(v).wait_send()

        entry_out(transit.at[v], v).wait_send()

        @pl.when(core == 1)
        def _():
            entry_on(v).wait_send()
            for n in range(3):
                share_out(1, v, n).wait_send()
                direct(v, n).wait_send()

        return carry

    lax.fori_loop(0, VECS, sent, 0)


def deal(tile, paired, energy, bias, mean):
    bias[...] = tile[0:WALKERS_DEV, 0:STOPS * VECS]
    paired[...] = tile[4, 0:WALKERS_DEV]
    energy[...] = tile[5, 0:WALKERS_DEV]
    mean[...] = tile[6, 0:1]


def body(chol, green, fields, weights_in, partner, counts):
    anywhere = pl.BlockSpec(memory_space=pl.ANY)
    vmem = pl.BlockSpec(memory_space=pltpu.VMEM)
    dma = pltpu.SemaphoreType.DMA
    tile = pltpu.VMEM((8, LANES), jnp.float32)
    out = pl.pallas_call(
        kernel,
        out_shape=jax.ShapeDtypeStruct((8, LANES), jnp.float32),
        in_specs=[anywhere] * 5 + [pl.BlockSpec(memory_space=pltpu.SMEM)],
        out_specs=vmem,
        scratch_shapes=[
            pltpu.VMEM((WALKERS_DEV, STOPS * VECS), jnp.float32),
            pltpu.SMEM((WALKERS_DEV,), jnp.float32),
            pltpu.SMEM((WALKERS_DEV,), jnp.int32),
            pltpu.VMEM((3, VECS, NOCC, ORB), jnp.bfloat16),
            pltpu.VMEM((2 * WALKERS_DEV, ORB, NOCC), jnp.bfloat16),
            pltpu.VMEM((NOCC, NOCC), jnp.float32),
            pltpu.VMEM((VECS, QUARTER, ORB), jnp.bfloat16),
            pltpu.VMEM((2 * VECS, 8, LANES), jnp.float32),
            pltpu.VMEM((8, 8, LANES), jnp.float32),
            tile, tile, tile, tile,
            pltpu.VMEM((16, 8, LANES), jnp.float32),
            pltpu.VMEM((8, 8, LANES), jnp.float32),
            dma((3,)), dma((2,)), dma((2,)), dma((2,)), dma((2,)),
            dma((2, VECS)), dma((2, VECS)), dma((VECS,)), dma((VECS,)),
            dma((2, VECS, 3)), dma((2, VECS, 3)), dma((VECS, 3)), dma((VECS, 3)),
            dma((2,)), dma((2,)), pltpu.SemaphoreType.REGULAR((3,)),
        ],
        compiler_params=pltpu.CompilerParams(
            collective_id=0, has_side_effects=True, vmem_limit_bytes=62 * 2**20
        ),
        name="walkers",
    )(chol, green, fields, weights_in, partner, counts)
    results = pl.pallas_call(
        deal,
        out_shape=(
            jax.ShapeDtypeStruct((WALKERS_DEV,), jnp.float32),
            jax.ShapeDtypeStruct((WALKERS_DEV,), jnp.float32),
            jax.ShapeDtypeStruct((WALKERS_DEV, STOPS * VECS), jnp.float32),
            jax.ShapeDtypeStruct((1,), jnp.float32),
        ),
        in_specs=[vmem],
        out_specs=(vmem,) * 4,
        name="deal",
    )(out)
    return results[0], results[1], results[2], results[3].reshape(())


def solution(mesh):
    placed = (
        P("ham", None, None),
        P(("walk", "ham"), None, None),
        P(("walk", "ham"), None),
        P(("walk", "ham")),
        P(("walk", "ham")),
        P("walk", "ham"),
    )
    return jax.shard_map(
        body,
        mesh=mesh,
        in_specs=placed,
        out_specs=(P(("walk", "ham")), P(("walk", "ham")), P(("walk", "ham"), None), P()),
        check_vma=False,
    )
```

```python
import functools

import jax
import jax.numpy as jnp
from jax import lax
from jax.experimental import pallas as pl
from jax.experimental.pallas import tpu as pltpu
from jax.sharding import PartitionSpec as P

ORB = 1024
NOCC = 256
VECS = 4
STOPS = 4
WALKERS_DEV = 4
QUARTER = NOCC // 4
EIGHTH = NOCC // 8
FIELD_COUPLING = 0.02
DRIFT_COST = 0.0002
ONE_BODY = 1.0
MESH = pl.DeviceIdType.MESH
LANES = 128
EXCH_LANE = 16
WEIGHT_LANE = 17
LIVE_LANE = 18
PLAN_0 = (
    "o0", "t0", "o1", "t1", "o2", "t2", "u0", "w0", "m0", "t3", "u1", "m1",
    "u2", "e0", "m2", "u3", "e1", "o3", "e2", "s0", "a0", "m3", "e3", "b0",
    "s1", "a1", "b1", "s2", "a2", "b2", "s3", "a3", "b3",
)
PLAN_1 = (
    "o0", "e0", "o1", "o2", "e1", "o3", "e2", "f0", "s0", "w0", "m0", "m1",
    "e3", "s1", "p0", "p1", "m2", "f1", "s2", "g0", "q0", "f2", "s3", "p2",
    "f3", "p3", "g1", "q1", "m3", "g2", "q2", "g3", "q3",
)


def rounds_of(plan, kinds):
    rounds, steps = [], {}
    order = list(kinds)
    for name in plan:
        kind = name[0]
        if kind in kinds:
            assert kind not in steps and all(order.index(k) < order.index(kind) for k in steps), name
            steps[kind] = int(name[1:])
        else:
            rounds.append((steps, name))
            steps = {}
    assert not steps
    return rounds


def product_terms(prod):
    a, b = prod[:128, :128], prod[:128, 128:]
    c, d = prod[128:, :128], prod[128:, 128:]
    i = lax.broadcasted_iota(jnp.int32, (128, 128), 0)
    j = lax.broadcasted_iota(jnp.int32, (128, 128), 1)
    low = jnp.where(i >= j, a, d)
    high = jnp.where(i < j, a, d)
    pairs = high * low.T + b * c.T
    gap = jnp.where(i == j, a - d, 0.0)
    diag = jnp.where(i == j, a + d, 0.0)
    exchange = jnp.sum((pairs + pairs + gap * gap).reshape(16, 8, 128), axis=0)
    trace = jnp.sum(diag, axis=0, keepdims=True)
    return trace, exchange


def kernel(
    chol, green, fields_in, weights_in, partner_in, counts, out,
    fields, weights, partner, vecs, theta, carry, transit, trace, exch, meta, meta_in, bias, bias_in, plane, line,
    small_sem, load_sem, theta_sem, meta_sem, bias_sem, entry_send, entry_recv, transit_send, transit_recv,
    share_send, share_recv, direct_send, direct_recv, plane_sem, line_sem, hail_sem,
):
    h, g = lax.axis_index("ham"), lax.axis_index("walk")
    z, y_hi, core = h // 4, lax.rem(h // 2, 2), lax.rem(h, 2)
    x, y_lo = g // 2, lax.rem(g, 2)
    y = y_hi * 2 + y_lo

    def device(x=x, y_hi=y_hi, y_lo=y_lo, z=z, core=core):
        return {"ham": z * 4 + y_hi * 2 + core, "walk": x * 2 + y_lo}

    sibling = device(core=1 - core)
    cross = device(y_hi=1 - y_hi, y_lo=1 - y_lo)
    twin = device(y_lo=1 - y_lo)
    x_up, x_down = device(x=lax.rem(x + 1, 4)), device(x=lax.rem(x + 3, 4))
    z_down = device(z=lax.rem(z + 7, 8))
    z_on = device(z=lax.rem(z + 9 - 2 * y_hi, 8))
    sharers = (x_down, x_up, twin)
    color = lax.rem(x + 2 * y_lo, 4)
    cross_color = lax.rem(x + 2 * (1 - y_lo), 4)
    colors = (lax.rem(color + 1, 4), lax.rem(color + 3, 4), lax.rem(color + 2, 4))

    def plane_peer(d):
        yy = lax.rem(y + d // 4, 4)
        return device(x=lax.rem(x + d % 4, 4), y_hi=yy // 2, y_lo=lax.rem(yy, 2))

    def line_peer(d):
        return device(z=lax.rem(z + d, 8))

    def quarter(k):
        return pl.ds(pl.multiple_of(k * QUARTER, QUARTER), QUARTER)

    def first(k):
        return pl.ds(pl.multiple_of(k * QUARTER, EIGHTH), EIGHTH)

    def second(k):
        return pl.ds(pl.multiple_of(k * QUARTER + EIGHTH, EIGHTH), EIGHTH)

    def remote(src, dst, send, recv, to):
        return pltpu.make_async_remote_copy(src, dst, send, recv, device_id=to, device_id_type=MESH)

    def hail(n):
        for peer in neighbours:
            pl.semaphore_signal(hail_sem.at[n], inc=1, device_id=peer, device_id_type=MESH)

    def heard(n):
        pl.semaphore_wait(hail_sem.at[n], 6)
        if n < 2:
            hail(n + 1)

    barrier = pltpu.get_barrier_semaphore()
    neighbours = (x_up, x_down, cross, twin, line_peer(1), line_peer(7))
    for peer in (sibling, *neighbours):
        pl.semaphore_signal(barrier, inc=1, device_id=peer, device_id_type=MESH)

    own_rows = pl.ds(core * WALKERS_DEV, WALKERS_DEV)
    small = [
        pltpu.make_async_copy(src, dst, small_sem.at[n])
        for n, (src, dst) in enumerate(
            ((fields_in, fields), (weights_in, weights), (partner_in, partner))
        )
    ]
    for copy in small:
        copy.start()
    load_slab = pltpu.make_async_copy(chol, vecs.at[0], load_sem.at[0])
    load_theta = pltpu.make_async_copy(green, theta.at[own_rows], load_sem.at[1])
    load_slab.start()
    load_theta.start()

    pl.semaphore_wait(barrier, 7)

    swap_theta = remote(green, theta.at[own_rows], theta_sem.at[0], theta_sem.at[1], sibling)
    swap_meta = remote(meta, meta_in, meta_sem.at[0], meta_sem.at[1], sibling)

    def entry_out(src, v):
        return remote(src, vecs.at[1, v, quarter(cross_color)], entry_send.at[0, v], entry_recv.at[0, v], cross)

    def entry_in(s, v):
        rows = vecs.at[1 + s, v, quarter(color)]
        return remote(rows, rows, entry_send.at[s, v], entry_recv.at[s, v], cross)

    def entry_on(v):
        rows = vecs.at[1, v, quarter(color)]
        return remote(rows, vecs.at[2, v, quarter(color)], entry_send.at[1, v], entry_recv.at[1, v], z_on)

    def transit_copy(v):
        return remote(chol.at[v, quarter(cross_color)], transit.at[v], transit_send.at[v], transit_recv.at[v], z_down)

    def part(s, k):
        return quarter(k) if s == 0 else first(k)

    def share_out(s, v, n):
        rows = vecs.at[1 + s, v, part(s, color)]
        return remote(rows, rows, share_send.at[s, v, n], share_recv.at[s, v, n], sharers[n])

    def share_in(s, v, n):
        rows = vecs.at[1 + s, v, part(s, colors[n])]
        return remote(rows, rows, share_send.at[s, v, n], share_recv.at[s, v, n], sharers[n])

    def direct(v, n):
        rows = second(colors[n])
        return remote(vecs.at[1, v, rows], vecs.at[2, v, rows], direct_send.at[v, n], direct_recv.at[v, n], z_on)

    row = lax.broadcasted_iota(jnp.int32, (8, LANES), 0)
    lane = lax.broadcasted_iota(jnp.int32, (8, LANES), 1)
    mine = row // 4 == core

    def prepare():
        for copy in small:
            copy.wait()
        meta[...] = jnp.zeros_like(meta)
        meta[0:4, 0:16] = fields[...]
        meta[4:8, 0:16] = fields[...]
        values = meta[...]
        for i in range(WALKERS_DEV):
            values = jnp.where((row % 4 == i) & (lane == WEIGHT_LANE), weights[i], values)
        values = jnp.where((row % 4 < counts[0, 0]) & (lane == LIVE_LANE), 1.0, values)
        meta[...] = jnp.where(mine, values, 0.0)
        exch[...] = jnp.zeros_like(exch)
        swap_meta.start()

    def note(slot, w, prod):
        diagonal, exchange = product_terms(prod)
        trace[slot, pl.ds(w, 1), :] = diagonal
        exch[w] += exchange

    def unit(s, v, base, last_slot, last_w):
        slot = jnp.where(s == 0, v, VECS + v)
        vector = vecs[s, v]
        note(last_slot, last_w, carry[...])
        for n in range(WALKERS_DEV):
            prod = jnp.dot(vector, theta[base + n], preferred_element_type=jnp.float32)
            if n < WALKERS_DEV - 1:
                note(slot, base + n, prod)
            else:
                carry[...] = prod
        return slot, base + WALKERS_DEV - 1

    mine_base, other_base = core * WALKERS_DEV, (1 - core) * WALKERS_DEV
    near_base = (1 - y_hi) * WALKERS_DEV
    next_base = y_hi * WALKERS_DEV

    def pass_on(v):
        @pl.when(y_hi == 0)
        def _():
            transit_copy(v).wait_recv()
            entry_out(transit.at[v], v).start()

    def send_on(v):
        @pl.when(y_hi == 1)
        def _():
            entry_out(chol.at[v, quarter(cross_color)], v).start()

    def enter(v):
        entry_in(0, v).wait_recv()
        for n in range(3):
            share_out(0, v, n).start()

    def enter_on(v):
        entry_in(0, v).wait_recv()
        entry_on(v).start()
        for n in range(3):
            share_out(0, v, n).start()

    def gather(v):
        for n in range(3):
            share_in(0, v, n).wait_recv()

    def gather_on(v):
        for n in range(3):
            share_in(0, v, n).wait_recv()
            direct(v, n).start()

    def second_enter(v):
        entry_in(1, v).wait_recv()
        for n in range(3):
            share_out(1, v, n).start()

    def second_gather(v):
        for n in range(3):
            share_in(1, v, n).wait_recv()
            direct(v, n).wait_recv()

    def swapped(v):
        swap_theta.wait_recv()

    def run(plan, steps, units):
        rounds = rounds_of(plan, steps)

        def round_(i, last):
            for n in range(3):
                pl.when(i == 3 * n + 2)(functools.partial(heard, n))

            for kind, action in steps.items():
                at = [(n, r[0][kind]) for n, r in enumerate(rounds) if kind in r[0]]
                if at:
                    v = sum(jnp.where(i == n, step, 0) for n, step in at)
                    hit = functools.reduce(jnp.logical_or, [i == n for n, _ in at])
                    pl.when(hit)(functools.partial(action, v))

            def pick(field):
                return sum(jnp.where(i == n, units(r[1])[field], 0) for n, r in enumerate(rounds))

            return unit(pick(0), pick(1), pick(2), *last)

        slot, w = lax.fori_loop(0, len(rounds), round_, (jnp.int32(0), jnp.int32(0)))
        note(slot, w, carry[...])

    own_units = {"o": (0, mine_base), "m": (0, other_base)}

    def unit_of(table):
        return lambda name: (table[name[0]][0], int(name[1:]), table[name[0]][1])

    carry[...] = jnp.zeros_like(carry)

    @pl.when(core == 0)
    def _():
        @pl.when(y_hi == 0)
        def _():
            for v in range(VECS):
                transit_copy(v).start()

        swap_theta.start()
        hail(0)
        prepare()
        load_slab.wait()
        load_theta.wait()
        steps = {"t": pass_on, "u": send_on, "e": enter, "s": gather, "w": swapped}
        run(PLAN_0, steps, unit_of(own_units | {"a": (1, mine_base), "b": (1, other_base)}))

    @pl.when(core == 1)
    def _():
        for v in range(VECS):
            entry_out(chol.at[v, quarter(cross_color)], v).start()
        swap_theta.start()
        hail(0)
        prepare()
        load_slab.wait()
        load_theta.wait()
        steps = {"e": enter_on, "f": second_enter, "s": gather_on, "g": second_gather, "w": swapped}
        run(PLAN_1, steps, unit_of(own_units | {"p": (1, near_base), "q": (2, next_base)}))

    lower = row < 4
    tile = jnp.zeros((8, LANES), jnp.float32)
    own_cols = jnp.where(lower, 4 + 4 * core, 4 * core)
    far_cols = jnp.where(lower, 12 - 12 * core, 8 + 4 * core)
    for slot in range(2 * VECS):
        cols = own_cols if slot < VECS else far_cols
        total = jnp.sum(trace[slot], axis=1, keepdims=True)
        tile = jnp.where(lane == cols + slot % VECS, total, tile)
    exch_rows = jnp.sum(exch[...], axis=1)
    tile = jnp.where(lane == EXCH_LANE, jnp.sum(exch_rows, axis=1, keepdims=True), tile)
    bias[...] = tile
    swap_bias = remote(bias, bias_in, bias_sem.at[0], bias_sem.at[1], sibling)
    swap_bias.start()
    swap_meta.wait_recv()
    known = meta[...] + meta_in[...]
    swap_bias.wait_recv()
    full = bias[...] + bias_in[...]
    is_bias = lane < STOPS * VECS

    def pick(keep, values):
        return jnp.sum(jnp.where(keep, values, 0.0), axis=1, keepdims=True)

    squares = pick(is_bias, full * full)
    drift = pick(is_bias, full * known)
    exchange = pick(lane == EXCH_LANE, full)
    energy = ONE_BODY + (0.5 * squares - 0.5 * exchange) / (NOCC * STOPS * VECS)
    weight = pick(lane == WEIGHT_LANE, known) * pick(lane == LIVE_LANE, known)
    weight = weight * jnp.exp(FIELD_COUPLING * drift - DRIFT_COST * squares)
    here = jnp.where(lane == 0, weight, jnp.where(lane == 1, weight * energy, 0.0))

    my_plane = x * 4 + y
    plane[my_plane] = here
    for d in (10, 9, 11, 6, 14, 5, 7, 13, 15, 2, 8, 1, 3, 4, 12):
        remote(plane.at[my_plane], plane.at[my_plane], plane_sem.at[0], plane_sem.at[1], plane_peer(d)).start()
    some = plane.at[pl.ds(0, 15)]
    remote(some, some, plane_sem.at[0], plane_sem.at[1], sibling).wait_recv()
    summed = plane[0]
    for n in range(1, 16):
        summed = summed + plane[n]
    line[z] = summed
    for d in (4, 3, 5, 2, 6, 1, 7):
        remote(line.at[z], line.at[z], line_sem.at[0], line_sem.at[1], line_peer(d)).start()

    table = jnp.zeros((8, LANES), jnp.float32)
    for n in range(8):
        column = plane[(n // 2) * 4 + y_hi * 2 + n % 2]
        table = jnp.where(lane == n, pick(lane == 0, column), table)
    mate = jnp.zeros((8, LANES), jnp.float32)
    for i in range(WALKERS_DEV):
        found = (row == core * 4 + (partner[i] & 3)) & (lane == partner[i] // (WALKERS_DEV * 32))
        value = jnp.sum(pick(found, table), axis=0, keepdims=True)
        mate = jnp.where(row % 4 == i, value, mate)
    paired = 0.5 * (weight + mate)

    some_line = line.at[pl.ds(0, 7)]
    remote(some_line, some_line, line_sem.at[0], line_sem.at[1], sibling).wait_recv()
    summed = line[0]
    for n in range(1, 8):
        summed = summed + line[n]
    totals = jnp.sum(summed, axis=0, keepdims=True)
    top = jnp.broadcast_to(totals, (8, LANES))
    mean = pick(lane == 1, top) / pick(lane == 0, top)
    eye = (row == lane) | (row == lane + 4)
    keep = eye & mine

    def along(values):
        return jnp.sum(jnp.where(keep, values, 0.0), axis=0, keepdims=True)

    biases = jnp.where(core == 0, full[0:4], full[4:8])
    out[0:4, :] = jnp.where(is_bias[0:4], biases, 0.0)
    out[4:5, :] = along(paired)
    out[5:6, :] = along(energy)
    out[6:7, :] = mean[0:1] + jnp.zeros((1, LANES), jnp.float32)

    remote(some, some, plane_sem.at[0], plane_sem.at[1], sibling).wait_send()
    remote(some_line, some_line, line_sem.at[0], line_sem.at[1], sibling).wait_send()
    swap_bias.wait_send()
    swap_theta.wait_send()
    swap_meta.wait_send()

    def sent(v, carry):
        for n in range(3):
            share_out(0, v, n).wait_send()

        @pl.when(core == 0)
        def _():
            @pl.when(y_hi == 0)
            def _():
                transit_copy(v).wait_send()

        entry_out(transit.at[v], v).wait_send()

        @pl.when(core == 1)
        def _():
            entry_on(v).wait_send()
            for n in range(3):
                share_out(1, v, n).wait_send()
                direct(v, n).wait_send()

        return carry

    lax.fori_loop(0, VECS, sent, 0)


def deal(tile, paired, energy, bias, mean):
    bias[...] = tile[0:WALKERS_DEV, 0:STOPS * VECS]
    paired[...] = tile[4, 0:WALKERS_DEV]
    energy[...] = tile[5, 0:WALKERS_DEV]
    mean[...] = tile[6, 0:1]


def body(chol, green, fields, weights_in, partner, counts):
    anywhere = pl.BlockSpec(memory_space=pl.ANY)
    vmem = pl.BlockSpec(memory_space=pltpu.VMEM)
    dma = pltpu.SemaphoreType.DMA
    tile = pltpu.VMEM((8, LANES), jnp.float32)
    out = pl.pallas_call(
        kernel,
        out_shape=jax.ShapeDtypeStruct((8, LANES), jnp.float32),
        in_specs=[anywhere] * 5 + [pl.BlockSpec(memory_space=pltpu.SMEM)],
        out_specs=vmem,
        scratch_shapes=[
            pltpu.VMEM((WALKERS_DEV, STOPS * VECS), jnp.float32),
            pltpu.SMEM((WALKERS_DEV,), jnp.float32),
            pltpu.SMEM((WALKERS_DEV,), jnp.int32),
            pltpu.VMEM((3, VECS, NOCC, ORB), jnp.bfloat16),
            pltpu.VMEM((2 * WALKERS_DEV, ORB, NOCC), jnp.bfloat16),
            pltpu.VMEM((NOCC, NOCC), jnp.float32),
            pltpu.VMEM((VECS, QUARTER, ORB), jnp.bfloat16),
            pltpu.VMEM((2 * VECS, 8, LANES), jnp.float32),
            pltpu.VMEM((8, 8, LANES), jnp.float32),
            tile, tile, tile, tile,
            pltpu.VMEM((16, 8, LANES), jnp.float32),
            pltpu.VMEM((8, 8, LANES), jnp.float32),
            dma((3,)), dma((2,)), dma((2,)), dma((2,)), dma((2,)),
            dma((2, VECS)), dma((2, VECS)), dma((VECS,)), dma((VECS,)),
            dma((2, VECS, 3)), dma((2, VECS, 3)), dma((VECS, 3)), dma((VECS, 3)),
            dma((2,)), dma((2,)), pltpu.SemaphoreType.REGULAR((3,)),
        ],
        compiler_params=pltpu.CompilerParams(
            collective_id=0, has_side_effects=True, vmem_limit_bytes=62 * 2**20
        ),
        name="walkers",
    )(chol, green, fields, weights_in, partner, counts)
    results = pl.pallas_call(
        deal,
        out_shape=(
            jax.ShapeDtypeStruct((WALKERS_DEV,), jnp.float32),
            jax.ShapeDtypeStruct((WALKERS_DEV,), jnp.float32),
            jax.ShapeDtypeStruct((WALKERS_DEV, STOPS * VECS), jnp.float32),
            jax.ShapeDtypeStruct((1,), jnp.float32),
        ),
        in_specs=[vmem],
        out_specs=(vmem,) * 4,
        name="deal",
    )(out)
    return results[0], results[1], results[2], results[3].reshape(())


def solution(mesh):
    placed = (
        P("ham", None, None),
        P(("walk", "ham"), None, None),
        P(("walk", "ham"), None),
        P(("walk", "ham")),
        P(("walk", "ham")),
        P("walk", "ham"),
    )
    return jax.shard_map(
        body,
        mesh=mesh,
        in_specs=placed,
        out_specs=(P(("walk", "ham")), P(("walk", "ham")), P(("walk", "ham"), None), P()),
        check_vma=False,
    )
```

```python
import functools

import jax
import jax.numpy as jnp
from jax import lax
from jax.experimental import pallas as pl
from jax.experimental.pallas import tpu as pltpu
from jax.sharding import PartitionSpec as P

ORB = 1024
NOCC = 256
VECS = 4
STOPS = 4
WALKERS_DEV = 4
QUARTER = NOCC // 4
EIGHTH = NOCC // 8
FIELD_COUPLING = 0.02
DRIFT_COST = 0.0002
ONE_BODY = 1.0
MESH = pl.DeviceIdType.MESH
LANES = 128
EXCH_LANE = 16
WEIGHT_LANE = 17
LIVE_LANE = 18
PLAN_0 = (
    "o0", "o1", "o2", "t0", "u0", "o3", "t1", "u1", "w0", "m0", "t2", "u2",
    "m1", "t3", "u3", "e0", "m2", "e1", "m3", "e2", "s0", "a0", "e3", "b0",
    "s1", "a1", "b1", "s2", "a2", "b2", "s3", "a3", "b3",
)
PLAN_1 = (
    "o0", "e0", "o1", "e1", "o2", "e2", "f0", "o3", "e3", "f1", "s0", "w0",
    "m0", "f2", "s1", "m1", "p0", "f3", "s2", "m2", "s3", "p1", "g0", "q0",
    "p2", "g1", "q1", "p3", "g2", "q2", "m3", "g3", "q3",
)


def rounds_of(plan, kinds):
    rounds, steps = [], {}
    order = list(kinds)
    for name in plan:
        kind = name[0]
        if kind in kinds:
            assert kind not in steps and all(order.index(k) < order.index(kind) for k in steps), name
            steps[kind] = int(name[1:])
        else:
            rounds.append((steps, name))
            steps = {}
    assert not steps
    return rounds


def product_terms(prod):
    a, b = prod[:128, :128], prod[:128, 128:]
    c, d = prod[128:, :128], prod[128:, 128:]
    i = lax.broadcasted_iota(jnp.int32, (128, 128), 0)
    j = lax.broadcasted_iota(jnp.int32, (128, 128), 1)
    low = jnp.where(i >= j, a, d)
    high = jnp.where(i < j, a, d)
    pairs = high * low.T + b * c.T
    gap = jnp.where(i == j, a - d, 0.0)
    diag = jnp.where(i == j, a + d, 0.0)
    exchange = jnp.sum((pairs + pairs + gap * gap).reshape(16, 8, 128), axis=0)
    trace = jnp.sum(diag, axis=0, keepdims=True)
    return trace, exchange


def kernel(
    chol, green, fields_in, weights_in, partner_in, counts, out,
    fields, weights, partner, vecs, theta, carry, transit, trace, exch, meta, meta_in, bias, bias_in, plane, line,
    small_sem, load_sem, theta_sem, meta_sem, bias_sem, entry_send, entry_recv, transit_send, transit_recv,
    share_send, share_recv, direct_send, direct_recv, plane_sem, line_sem, hail_sem,
):
    h, g = lax.axis_index("ham"), lax.axis_index("walk")
    z, y_hi, core = h // 4, lax.rem(h // 2, 2), lax.rem(h, 2)
    x, y_lo = g // 2, lax.rem(g, 2)
    y = y_hi * 2 + y_lo

    def device(x=x, y_hi=y_hi, y_lo=y_lo, z=z, core=core):
        return {"ham": z * 4 + y_hi * 2 + core, "walk": x * 2 + y_lo}

    sibling = device(core=1 - core)
    cross = device(y_hi=1 - y_hi, y_lo=1 - y_lo)
    twin = device(y_lo=1 - y_lo)
    x_up, x_down = device(x=lax.rem(x + 1, 4)), device(x=lax.rem(x + 3, 4))
    z_down = device(z=lax.rem(z + 7, 8))
    z_on = device(z=lax.rem(z + 9 - 2 * y_hi, 8))
    sharers = (x_down, x_up, twin)
    color = lax.rem(x + 2 * y_lo, 4)
    cross_color = lax.rem(x + 2 * (1 - y_lo), 4)
    colors = (lax.rem(color + 1, 4), lax.rem(color + 3, 4), lax.rem(color + 2, 4))

    def plane_peer(d):
        yy = lax.rem(y + d // 4, 4)
        return device(x=lax.rem(x + d % 4, 4), y_hi=yy // 2, y_lo=lax.rem(yy, 2))

    def line_peer(d):
        return device(z=lax.rem(z + d, 8))

    def quarter(k):
        return pl.ds(pl.multiple_of(k * QUARTER, QUARTER), QUARTER)

    def first(k):
        return pl.ds(pl.multiple_of(k * QUARTER, EIGHTH), EIGHTH)

    def second(k):
        return pl.ds(pl.multiple_of(k * QUARTER + EIGHTH, EIGHTH), EIGHTH)

    def remote(src, dst, send, recv, to):
        return pltpu.make_async_remote_copy(src, dst, send, recv, device_id=to, device_id_type=MESH)

    def hail(n):
        for peer in neighbours:
            pl.semaphore_signal(hail_sem.at[n], inc=1, device_id=peer, device_id_type=MESH)

    def heard(n):
        pl.semaphore_wait(hail_sem.at[n], 6)
        if n < 2:
            hail(n + 1)

    barrier = pltpu.get_barrier_semaphore()
    neighbours = (x_up, x_down, cross, twin, line_peer(1), line_peer(7))
    for peer in (sibling, *neighbours):
        pl.semaphore_signal(barrier, inc=1, device_id=peer, device_id_type=MESH)

    own_rows = pl.ds(core * WALKERS_DEV, WALKERS_DEV)
    small = [
        pltpu.make_async_copy(src, dst, small_sem.at[n])
        for n, (src, dst) in enumerate(
            ((fields_in, fields), (weights_in, weights), (partner_in, partner))
        )
    ]
    for copy in small:
        copy.start()
    load_slab = pltpu.make_async_copy(chol, vecs.at[0], load_sem.at[0])
    load_theta = pltpu.make_async_copy(green, theta.at[own_rows], load_sem.at[1])

    pl.semaphore_wait(barrier, 7)

    swap_theta = remote(green, theta.at[own_rows], theta_sem.at[0], theta_sem.at[1], sibling)
    swap_meta = remote(meta, meta_in, meta_sem.at[0], meta_sem.at[1], sibling)

    def entry_out(src, v):
        return remote(src, vecs.at[1, v, quarter(cross_color)], entry_send.at[0, v], entry_recv.at[0, v], cross)

    def entry_in(s, v):
        rows = vecs.at[1 + s, v, quarter(color)]
        return remote(rows, rows, entry_send.at[s, v], entry_recv.at[s, v], cross)

    def entry_on(v):
        rows = vecs.at[1, v, quarter(color)]
        return remote(rows, vecs.at[2, v, quarter(color)], entry_send.at[1, v], entry_recv.at[1, v], z_on)

    def transit_copy(v):
        return remote(chol.at[v, quarter(cross_color)], transit.at[v], transit_send.at[v], transit_recv.at[v], z_down)

    def part(s, k):
        return quarter(k) if s == 0 else first(k)

    def share_out(s, v, n):
        rows = vecs.at[1 + s, v, part(s, color)]
        return remote(rows, rows, share_send.at[s, v, n], share_recv.at[s, v, n], sharers[n])

    def share_in(s, v, n):
        rows = vecs.at[1 + s, v, part(s, colors[n])]
        return remote(rows, rows, share_send.at[s, v, n], share_recv.at[s, v, n], sharers[n])

    def direct(v, n):
        rows = second(colors[n])
        return remote(vecs.at[1, v, rows], vecs.at[2, v, rows], direct_send.at[v, n], direct_recv.at[v, n], z_on)

    row = lax.broadcasted_iota(jnp.int32, (8, LANES), 0)
    lane = lax.broadcasted_iota(jnp.int32, (8, LANES), 1)
    mine = row // 4 == core

    def prepare():
        for copy in small:
            copy.wait()
        meta[...] = jnp.zeros_like(meta)
        meta[0:4, 0:16] = fields[...]
        meta[4:8, 0:16] = fields[...]
        values = meta[...]
        for i in range(WALKERS_DEV):
            values = jnp.where((row % 4 == i) & (lane == WEIGHT_LANE), weights[i], values)
        values = jnp.where((row % 4 < counts[0, 0]) & (lane == LIVE_LANE), 1.0, values)
        meta[...] = jnp.where(mine, values, 0.0)
        exch[...] = jnp.zeros_like(exch)
        swap_meta.start()

    def note(slot, w, prod):
        diagonal, exchange = product_terms(prod)
        trace[slot, pl.ds(w, 1), :] = diagonal
        exch[w] += exchange

    def unit(s, v, base, last_slot, last_w):
        slot = jnp.where(s == 0, v, VECS + v)
        vector = vecs[s, v]
        note(last_slot, last_w, carry[...])
        for n in range(WALKERS_DEV):
            prod = jnp.dot(vector, theta[base + n], preferred_element_type=jnp.float32)
            if n < WALKERS_DEV - 1:
                note(slot, base + n, prod)
            else:
                carry[...] = prod
        return slot, base + WALKERS_DEV - 1

    mine_base, other_base = core * WALKERS_DEV, (1 - core) * WALKERS_DEV
    near_base = (1 - y_hi) * WALKERS_DEV
    next_base = y_hi * WALKERS_DEV

    def pass_on(v):
        @pl.when(y_hi == 0)
        def _():
            transit_copy(v).wait_recv()
            entry_out(transit.at[v], v).start()

    def send_on(v):
        @pl.when(y_hi == 1)
        def _():
            entry_out(chol.at[v, quarter(cross_color)], v).start()

    def enter(v):
        entry_in(0, v).wait_recv()
        for n in range(3):
            share_out(0, v, n).start()

    def enter_on(v):
        entry_in(0, v).wait_recv()
        entry_on(v).start()
        for n in range(3):
            share_out(0, v, n).start()

    def gather(v):
        for n in range(3):
            share_in(0, v, n).wait_recv()

    def gather_on(v):
        for n in range(3):
            share_in(0, v, n).wait_recv()
            direct(v, n).start()

    def second_enter(v):
        entry_in(1, v).wait_recv()
        for n in range(3):
            share_out(1, v, n).start()

    def second_gather(v):
        for n in range(3):
            share_in(1, v, n).wait_recv()
            direct(v, n).wait_recv()

    def swapped(v):
        swap_theta.wait_recv()

    def run(plan, steps, units):
        rounds = rounds_of(plan, steps)

        def round_(i, last):
            for n in range(3):
                pl.when(i == 3 * n + 2)(functools.partial(heard, n))

            for kind, action in steps.items():
                at = [(n, r[0][kind]) for n, r in enumerate(rounds) if kind in r[0]]
                if at:
                    v = sum(jnp.where(i == n, step, 0) for n, step in at)
                    hit = functools.reduce(jnp.logical_or, [i == n for n, _ in at])
                    pl.when(hit)(functools.partial(action, v))

            def pick(field):
                return sum(jnp.where(i == n, units(r[1])[field], 0) for n, r in enumerate(rounds))

            return unit(pick(0), pick(1), pick(2), *last)

        slot, w = lax.fori_loop(0, len(rounds), round_, (jnp.int32(0), jnp.int32(0)))
        note(slot, w, carry[...])

    own_units = {"o": (0, mine_base), "m": (0, other_base)}

    def unit_of(table):
        return lambda name: (table[name[0]][0], int(name[1:]), table[name[0]][1])

    carry[...] = jnp.zeros_like(carry)

    @pl.when(core == 0)
    def _():
        @pl.when(y_hi == 0)
        def _():
            for v in range(VECS):
                transit_copy(v).start()

        swap_theta.start()
        load_slab.start()
        load_theta.start()
        hail(0)
        prepare()
        load_slab.wait()
        load_theta.wait()
        steps = {"t": pass_on, "u": send_on, "e": enter, "s": gather, "w": swapped}
        run(PLAN_0, steps, unit_of(own_units | {"a": (1, mine_base), "b": (1, other_base)}))

    @pl.when(core == 1)
    def _():
        for v in range(VECS):
            entry_out(chol.at[v, quarter(cross_color)], v).start()
        swap_theta.start()
        load_slab.start()
        load_theta.start()
        hail(0)
        prepare()
        load_slab.wait()
        load_theta.wait()
        steps = {"e": enter_on, "f": second_enter, "s": gather_on, "g": second_gather, "w": swapped}
        run(PLAN_1, steps, unit_of(own_units | {"p": (1, near_base), "q": (2, next_base)}))

    lower = row < 4
    tile = jnp.zeros((8, LANES), jnp.float32)
    own_cols = jnp.where(lower, 4 + 4 * core, 4 * core)
    far_cols = jnp.where(lower, 12 - 12 * core, 8 + 4 * core)
    for slot in range(2 * VECS):
        cols = own_cols if slot < VECS else far_cols
        total = jnp.sum(trace[slot], axis=1, keepdims=True)
        tile = jnp.where(lane == cols + slot % VECS, total, tile)
    exch_rows = jnp.sum(exch[...], axis=1)
    tile = jnp.where(lane == EXCH_LANE, jnp.sum(exch_rows, axis=1, keepdims=True), tile)
    bias[...] = tile
    swap_bias = remote(bias, bias_in, bias_sem.at[0], bias_sem.at[1], sibling)
    swap_bias.start()
    swap_meta.wait_recv()
    known = meta[...] + meta_in[...]
    swap_bias.wait_recv()
    full = bias[...] + bias_in[...]
    is_bias = lane < STOPS * VECS

    def pick(keep, values):
        return jnp.sum(jnp.where(keep, values, 0.0), axis=1, keepdims=True)

    squares = pick(is_bias, full * full)
    drift = pick(is_bias, full * known)
    exchange = pick(lane == EXCH_LANE, full)
    energy = ONE_BODY + (0.5 * squares - 0.5 * exchange) / (NOCC * STOPS * VECS)
    weight = pick(lane == WEIGHT_LANE, known) * pick(lane == LIVE_LANE, known)
    weight = weight * jnp.exp(FIELD_COUPLING * drift - DRIFT_COST * squares)
    spread = jnp.where((row == lane) | (lane == 8), weight, jnp.where(lane == 9, weight * energy, 0.0))
    here = jnp.sum(spread, axis=0, keepdims=True)

    my_plane = x * 4 + y
    plane[my_plane] = here
    for d in (10, 9, 11, 6, 14, 5, 7, 13, 15, 2, 8, 1, 3, 4, 12):
        remote(plane.at[my_plane], plane.at[my_plane], plane_sem.at[0], plane_sem.at[1], plane_peer(d)).start()
    some = plane.at[pl.ds(0, 15)]
    remote(some, some, plane_sem.at[0], plane_sem.at[1], sibling).wait_recv()
    summed = plane[0]
    for n in range(1, 16):
        summed = summed + plane[n]
    line[z] = summed
    for d in (4, 3, 5, 2, 6, 1, 7):
        remote(line.at[z], line.at[z], line_sem.at[0], line_sem.at[1], line_peer(d)).start()

    remote(some, some, plane_sem.at[0], plane_sem.at[1], sibling).wait_send()
    swap_bias.wait_send()
    swap_theta.wait_send()
    swap_meta.wait_send()

    def sent(v, carry):
        for n in range(3):
            share_out(0, v, n).wait_send()

        @pl.when(core == 0)
        def _():
            @pl.when(y_hi == 0)
            def _():
                transit_copy(v).wait_send()

        entry_out(transit.at[v], v).wait_send()

        @pl.when(core == 1)
        def _():
            entry_on(v).wait_send()
            for n in range(3):
                share_out(1, v, n).wait_send()
                direct(v, n).wait_send()

        return carry

    lax.fori_loop(0, VECS, sent, 0)

    table = jnp.zeros((8, LANES), jnp.float32)
    for n in range(8):
        table = jnp.where(row == n, plane[(n // 2) * 4 + y_hi * 2 + n % 2], table)
    mate = jnp.zeros((8, LANES), jnp.float32)
    for i in range(WALKERS_DEV):
        found = (row == partner[i] // (WALKERS_DEV * 32)) & (lane == core * 4 + (partner[i] & 3))
        value = jnp.sum(pick(found, table), axis=0, keepdims=True)
        mate = jnp.where(row % 4 == i, value, mate)
    paired = 0.5 * (weight + mate)

    some_line = line.at[pl.ds(0, 7)]
    remote(some_line, some_line, line_sem.at[0], line_sem.at[1], sibling).wait_recv()
    summed = line[0]
    for n in range(1, 8):
        summed = summed + line[n]
    top = jnp.broadcast_to(summed, (8, LANES))
    mean = pick(lane == 9, top) / pick(lane == 8, top)
    eye = (row == lane) | (row == lane + 4)
    keep = eye & mine

    def along(values):
        return jnp.sum(jnp.where(keep, values, 0.0), axis=0, keepdims=True)

    biases = jnp.where(core == 0, full[0:4], full[4:8])
    out[0:4, :] = jnp.where(is_bias[0:4], biases, 0.0)
    out[4:5, :] = along(paired)
    out[5:6, :] = along(energy)
    out[6:7, :] = mean[0:1] + jnp.zeros((1, LANES), jnp.float32)

    remote(some_line, some_line, line_sem.at[0], line_sem.at[1], sibling).wait_send()


def deal(tile, paired, energy, bias, mean):
    bias[...] = tile[0:WALKERS_DEV, 0:STOPS * VECS]
    paired[...] = tile[4, 0:WALKERS_DEV]
    energy[...] = tile[5, 0:WALKERS_DEV]
    mean[...] = tile[6, 0:1]


def body(chol, green, fields, weights_in, partner, counts):
    anywhere = pl.BlockSpec(memory_space=pl.ANY)
    vmem = pl.BlockSpec(memory_space=pltpu.VMEM)
    dma = pltpu.SemaphoreType.DMA
    tile = pltpu.VMEM((8, LANES), jnp.float32)
    out = pl.pallas_call(
        kernel,
        out_shape=jax.ShapeDtypeStruct((8, LANES), jnp.float32),
        in_specs=[anywhere] * 5 + [pl.BlockSpec(memory_space=pltpu.SMEM)],
        out_specs=vmem,
        scratch_shapes=[
            pltpu.VMEM((WALKERS_DEV, STOPS * VECS), jnp.float32),
            pltpu.SMEM((WALKERS_DEV,), jnp.float32),
            pltpu.SMEM((WALKERS_DEV,), jnp.int32),
            pltpu.VMEM((3, VECS, NOCC, ORB), jnp.bfloat16),
            pltpu.VMEM((2 * WALKERS_DEV, ORB, NOCC), jnp.bfloat16),
            pltpu.VMEM((NOCC, NOCC), jnp.float32),
            pltpu.VMEM((VECS, QUARTER, ORB), jnp.bfloat16),
            pltpu.VMEM((2 * VECS, 8, LANES), jnp.float32),
            pltpu.VMEM((8, 8, LANES), jnp.float32),
            tile, tile, tile, tile,
            pltpu.VMEM((16, 1, LANES), jnp.float32),
            pltpu.VMEM((8, 1, LANES), jnp.float32),
            dma((3,)), dma((2,)), dma((2,)), dma((2,)), dma((2,)),
            dma((2, VECS)), dma((2, VECS)), dma((VECS,)), dma((VECS,)),
            dma((2, VECS, 3)), dma((2, VECS, 3)), dma((VECS, 3)), dma((VECS, 3)),
            dma((2,)), dma((2,)), pltpu.SemaphoreType.REGULAR((3,)),
        ],
        compiler_params=pltpu.CompilerParams(
            collective_id=0, has_side_effects=True, vmem_limit_bytes=62 * 2**20
        ),
        name="walkers",
    )(chol, green, fields, weights_in, partner, counts)
    results = pl.pallas_call(
        deal,
        out_shape=(
            jax.ShapeDtypeStruct((WALKERS_DEV,), jnp.float32),
            jax.ShapeDtypeStruct((WALKERS_DEV,), jnp.float32),
            jax.ShapeDtypeStruct((WALKERS_DEV, STOPS * VECS), jnp.float32),
            jax.ShapeDtypeStruct((1,), jnp.float32),
        ),
        in_specs=[vmem],
        out_specs=(vmem,) * 4,
        name="deal",
    )(out)
    return results[0], results[1], results[2], results[3].reshape(())


def solution(mesh):
    placed = (
        P("ham", None, None),
        P(("walk", "ham"), None, None),
        P(("walk", "ham"), None),
        P(("walk", "ham")),
        P(("walk", "ham")),
        P("walk", "ham"),
    )
    return jax.shard_map(
        body,
        mesh=mesh,
        in_specs=placed,
        out_specs=(P(("walk", "ham")), P(("walk", "ham")), P(("walk", "ham"), None), P()),
        check_vma=False,
    )
```

```python
import functools

import jax
import jax.numpy as jnp
from jax import lax
from jax.experimental import pallas as pl
from jax.experimental.pallas import tpu as pltpu
from jax.sharding import PartitionSpec as P

ORB = 1024
NOCC = 256
VECS = 4
STOPS = 4
WALKERS_DEV = 4
QUARTER = NOCC // 4
EIGHTH = NOCC // 8
FIELD_COUPLING = 0.02
DRIFT_COST = 0.0002
ONE_BODY = 1.0
MESH = pl.DeviceIdType.MESH
LANES = 128
EXCH_LANE = 16
WEIGHT_LANE = 17
LIVE_LANE = 18
PLAN_0 = (
    "o0", "o1", "o2", "t0", "u0", "o3", "t1", "u1", "w0", "m0", "t2", "u2",
    "m1", "t3", "u3", "e0", "m2", "e1", "m3", "e2", "s0", "a0", "e3", "b0",
    "s1", "a1", "b1", "s2", "a2", "b2", "s3", "a3", "b3",
)
PLAN_1 = (
    "o0", "e0", "o1", "e1", "o2", "e2", "f0", "o3", "e3", "f1", "s0", "w0",
    "m0", "f2", "s1", "m1", "p0", "f3", "s2", "m2", "s3", "p1", "g0", "q0",
    "p2", "g1", "q1", "p3", "g2", "q2", "m3", "g3", "q3",
)


def rounds_of(plan, kinds):
    rounds, steps = [], {}
    order = list(kinds)
    for name in plan:
        kind = name[0]
        if kind in kinds:
            assert kind not in steps and all(order.index(k) < order.index(kind) for k in steps), name
            steps[kind] = int(name[1:])
        else:
            rounds.append((steps, name))
            steps = {}
    assert not steps
    return rounds


def product_terms(prod):
    a, b = prod[:128, :128], prod[:128, 128:]
    c, d = prod[128:, :128], prod[128:, 128:]
    i = lax.broadcasted_iota(jnp.int32, (128, 128), 0)
    j = lax.broadcasted_iota(jnp.int32, (128, 128), 1)
    low = jnp.where(i >= j, a, d)
    high = jnp.where(i < j, a, d)
    pairs = high * low.T + b * c.T
    gap = jnp.where(i == j, a - d, 0.0)
    diag = jnp.where(i == j, a + d, 0.0)
    exchange = jnp.sum((pairs + pairs + gap * gap).reshape(16, 8, 128), axis=0)
    trace = jnp.sum(diag, axis=0, keepdims=True)
    return trace, exchange


def kernel(
    chol, green, fields_in, weights_in, partner_in, counts, out,
    fields, weights, partner, vecs, theta, carry, transit, trace, exch, meta, meta_in, bias, bias_in, plane, line,
    small_sem, load_sem, theta_sem, meta_sem, bias_sem, entry_send, entry_recv, transit_send, transit_recv,
    share_send, share_recv, direct_send, direct_recv, plane_sem, line_sem, hail_sem,
):
    h, g = lax.axis_index("ham"), lax.axis_index("walk")
    z, y_hi, core = h // 4, lax.rem(h // 2, 2), lax.rem(h, 2)
    x, y_lo = g // 2, lax.rem(g, 2)
    y = y_hi * 2 + y_lo

    def device(x=x, y_hi=y_hi, y_lo=y_lo, z=z, core=core):
        return {"ham": z * 4 + y_hi * 2 + core, "walk": x * 2 + y_lo}

    sibling = device(core=1 - core)
    cross = device(y_hi=1 - y_hi, y_lo=1 - y_lo)
    twin = device(y_lo=1 - y_lo)
    x_up, x_down = device(x=lax.rem(x + 1, 4)), device(x=lax.rem(x + 3, 4))
    z_down = device(z=lax.rem(z + 7, 8))
    z_on = device(z=lax.rem(z + 9 - 2 * y_hi, 8))
    sharers = (x_down, x_up, twin)
    color = lax.rem(x + 2 * y_lo, 4)
    cross_color = lax.rem(x + 2 * (1 - y_lo), 4)
    colors = (lax.rem(color + 1, 4), lax.rem(color + 3, 4), lax.rem(color + 2, 4))

    def plane_peer(d):
        yy = lax.rem(y + d // 4, 4)
        return device(x=lax.rem(x + d % 4, 4), y_hi=yy // 2, y_lo=lax.rem(yy, 2))

    def line_peer(d):
        return device(z=lax.rem(z + d, 8))

    def quarter(k):
        return pl.ds(pl.multiple_of(k * QUARTER, QUARTER), QUARTER)

    def first(k):
        return pl.ds(pl.multiple_of(k * QUARTER, EIGHTH), EIGHTH)

    def second(k):
        return pl.ds(pl.multiple_of(k * QUARTER + EIGHTH, EIGHTH), EIGHTH)

    def remote(src, dst, send, recv, to):
        return pltpu.make_async_remote_copy(src, dst, send, recv, device_id=to, device_id_type=MESH)

    def hail(n):
        for peer in neighbours:
            pl.semaphore_signal(hail_sem.at[n], inc=1, device_id=peer, device_id_type=MESH)

    def heard(n):
        pl.semaphore_wait(hail_sem.at[n], 6)
        if n < 2:
            hail(n + 1)

    barrier = pltpu.get_barrier_semaphore()
    neighbours = (x_up, x_down, cross, twin, line_peer(1), line_peer(7))
    for peer in (sibling, *neighbours):
        pl.semaphore_signal(barrier, inc=1, device_id=peer, device_id_type=MESH)

    own_rows = pl.ds(core * WALKERS_DEV, WALKERS_DEV)
    small = [
        pltpu.make_async_copy(src, dst, small_sem.at[n])
        for n, (src, dst) in enumerate(
            ((fields_in, fields), (weights_in, weights), (partner_in, partner))
        )
    ]
    for copy in small:
        copy.start()
    load_slab = pltpu.make_async_copy(chol, vecs.at[0], load_sem.at[0])
    load_theta = pltpu.make_async_copy(green, theta.at[own_rows], load_sem.at[1])

    pl.semaphore_wait(barrier, 7)

    swap_theta = remote(theta.at[own_rows], theta.at[own_rows], theta_sem.at[0], theta_sem.at[1], sibling)
    swap_meta = remote(meta, meta_in, meta_sem.at[0], meta_sem.at[1], sibling)

    def entry_out(src, v):
        return remote(src, vecs.at[1, v, quarter(cross_color)], entry_send.at[0, v], entry_recv.at[0, v], cross)

    def entry_in(s, v):
        rows = vecs.at[1 + s, v, quarter(color)]
        return remote(rows, rows, entry_send.at[s, v], entry_recv.at[s, v], cross)

    def entry_on(v):
        rows = vecs.at[1, v, quarter(color)]
        return remote(rows, vecs.at[2, v, quarter(color)], entry_send.at[1, v], entry_recv.at[1, v], z_on)

    def transit_copy(v):
        return remote(chol.at[v, quarter(cross_color)], transit.at[v], transit_send.at[v], transit_recv.at[v], z_down)

    def part(s, k):
        return quarter(k) if s == 0 else first(k)

    def share_out(s, v, n):
        rows = vecs.at[1 + s, v, part(s, color)]
        return remote(rows, rows, share_send.at[s, v, n], share_recv.at[s, v, n], sharers[n])

    def share_in(s, v, n):
        rows = vecs.at[1 + s, v, part(s, colors[n])]
        return remote(rows, rows, share_send.at[s, v, n], share_recv.at[s, v, n], sharers[n])

    def direct(v, n):
        rows = second(colors[n])
        return remote(vecs.at[1, v, rows], vecs.at[2, v, rows], direct_send.at[v, n], direct_recv.at[v, n], z_on)

    row = lax.broadcasted_iota(jnp.int32, (8, LANES), 0)
    lane = lax.broadcasted_iota(jnp.int32, (8, LANES), 1)
    mine = row // 4 == core

    def prepare():
        for copy in small:
            copy.wait()
        meta[...] = jnp.zeros_like(meta)
        meta[0:4, 0:16] = fields[...]
        meta[4:8, 0:16] = fields[...]
        values = meta[...]
        for i in range(WALKERS_DEV):
            values = jnp.where((row % 4 == i) & (lane == WEIGHT_LANE), weights[i], values)
        values = jnp.where((row % 4 < counts[0, 0]) & (lane == LIVE_LANE), 1.0, values)
        meta[...] = jnp.where(mine, values, 0.0)
        exch[...] = jnp.zeros_like(exch)
        swap_meta.start()

    def note(slot, w, prod):
        diagonal, exchange = product_terms(prod)
        trace[slot, pl.ds(w, 1), :] = diagonal
        exch[w] += exchange

    def unit(s, v, base, last_slot, last_w):
        slot = jnp.where(s == 0, v, VECS + v)
        vector = vecs[s, v]
        note(last_slot, last_w, carry[...])
        for n in range(WALKERS_DEV):
            prod = jnp.dot(vector, theta[base + n], preferred_element_type=jnp.float32)
            if n < WALKERS_DEV - 1:
                note(slot, base + n, prod)
            else:
                carry[...] = prod
        return slot, base + WALKERS_DEV - 1

    mine_base, other_base = core * WALKERS_DEV, (1 - core) * WALKERS_DEV
    near_base = (1 - y_hi) * WALKERS_DEV
    next_base = y_hi * WALKERS_DEV

    def pass_on(v):
        @pl.when(y_hi == 0)
        def _():
            transit_copy(v).wait_recv()
            entry_out(transit.at[v], v).start()

    def send_on(v):
        @pl.when(y_hi == 1)
        def _():
            entry_out(chol.at[v, quarter(cross_color)], v).start()

    def enter(v):
        entry_in(0, v).wait_recv()
        for n in range(3):
            share_out(0, v, n).start()

    def enter_on(v):
        entry_in(0, v).wait_recv()
        for n in range(3):
            share_out(0, v, n).start()
        entry_on(v).start()

    def gather(v):
        for n in range(3):
            share_in(0, v, n).wait_recv()

    def gather_on(v):
        for n in range(3):
            share_in(0, v, n).wait_recv()
            direct(v, n).start()

    def second_enter(v):
        entry_in(1, v).wait_recv()
        for n in range(3):
            share_out(1, v, n).start()

    def second_gather(v):
        for n in range(3):
            share_in(1, v, n).wait_recv()
            direct(v, n).wait_recv()

    def swapped(v):
        swap_theta.wait_recv()

    def run(plan, steps, units):
        rounds = rounds_of(plan, steps)

        def round_(i, last):
            for n in range(3):
                pl.when(i == 3 * n + 2)(functools.partial(heard, n))

            for kind, action in steps.items():
                at = [(n, r[0][kind]) for n, r in enumerate(rounds) if kind in r[0]]
                if at:
                    v = sum(jnp.where(i == n, step, 0) for n, step in at)
                    hit = functools.reduce(jnp.logical_or, [i == n for n, _ in at])
                    pl.when(hit)(functools.partial(action, v))

            def pick(field):
                return sum(jnp.where(i == n, units(r[1])[field], 0) for n, r in enumerate(rounds))

            return unit(pick(0), pick(1), pick(2), *last)

        slot, w = lax.fori_loop(0, len(rounds), round_, (jnp.int32(0), jnp.int32(0)))
        note(slot, w, carry[...])

    own_units = {"o": (0, mine_base), "m": (0, other_base)}

    def unit_of(table):
        return lambda name: (table[name[0]][0], int(name[1:]), table[name[0]][1])

    carry[...] = jnp.zeros_like(carry)

    @pl.when(core == 0)
    def _():
        @pl.when(y_hi == 0)
        def _():
            for v in range(VECS):
                transit_copy(v).start()

        load_theta.start()
        load_slab.start()
        hail(0)
        prepare()
        load_theta.wait()
        swap_theta.start()
        load_slab.wait()
        steps = {"t": pass_on, "u": send_on, "e": enter, "s": gather, "w": swapped}
        run(PLAN_0, steps, unit_of(own_units | {"a": (1, mine_base), "b": (1, other_base)}))

    @pl.when(core == 1)
    def _():
        for v in range(VECS):
            entry_out(chol.at[v, quarter(cross_color)], v).start()
        load_theta.start()
        load_slab.start()
        hail(0)
        prepare()
        load_theta.wait()
        swap_theta.start()
        load_slab.wait()
        steps = {"e": enter_on, "f": second_enter, "s": gather_on, "g": second_gather, "w": swapped}
        run(PLAN_1, steps, unit_of(own_units | {"p": (1, near_base), "q": (2, next_base)}))

    lower = row < 4
    tile = jnp.zeros((8, LANES), jnp.float32)
    own_cols = jnp.where(lower, 4 + 4 * core, 4 * core)
    far_cols = jnp.where(lower, 12 - 12 * core, 8 + 4 * core)
    for slot in range(2 * VECS):
        cols = own_cols if slot < VECS else far_cols
        total = jnp.sum(trace[slot], axis=1, keepdims=True)
        tile = jnp.where(lane == cols + slot % VECS, total, tile)
    exch_rows = jnp.sum(exch[...], axis=1)
    tile = jnp.where(lane == EXCH_LANE, jnp.sum(exch_rows, axis=1, keepdims=True), tile)
    bias[...] = tile
    swap_bias = remote(bias, bias_in, bias_sem.at[0], bias_sem.at[1], sibling)
    swap_bias.start()
    swap_meta.wait_recv()
    known = meta[...] + meta_in[...]
    swap_bias.wait_recv()
    full = bias[...] + bias_in[...]
    is_bias = lane < STOPS * VECS

    def pick(keep, values):
        return jnp.sum(jnp.where(keep, values, 0.0), axis=1, keepdims=True)

    squares = pick(is_bias, full * full)
    drift = pick(is_bias, full * known)
    exchange = pick(lane == EXCH_LANE, full)
    energy = ONE_BODY + (0.5 * squares - 0.5 * exchange) / (NOCC * STOPS * VECS)
    weight = pick(lane == WEIGHT_LANE, known) * pick(lane == LIVE_LANE, known)
    weight = weight * jnp.exp(FIELD_COUPLING * drift - DRIFT_COST * squares)
    spread = jnp.where((row == lane) | (lane == 8), weight, jnp.where(lane == 9, weight * energy, 0.0))
    here = jnp.sum(spread, axis=0, keepdims=True)

    my_plane = x * 4 + y
    plane[my_plane] = here
    for d in (10, 9, 11, 6, 14, 5, 7, 13, 15, 2, 8, 1, 3, 4, 12):
        remote(plane.at[my_plane], plane.at[my_plane], plane_sem.at[0], plane_sem.at[1], plane_peer(d)).start()
    some = plane.at[pl.ds(0, 15)]
    remote(some, some, plane_sem.at[0], plane_sem.at[1], sibling).wait_recv()
    summed = plane[0]
    for n in range(1, 16):
        summed = summed + plane[n]
    line[z] = summed
    for d in (4, 3, 5, 2, 6, 1, 7):
        remote(line.at[z], line.at[z], line_sem.at[0], line_sem.at[1], line_peer(d)).start()

    remote(some, some, plane_sem.at[0], plane_sem.at[1], sibling).wait_send()
    swap_bias.wait_send()
    swap_theta.wait_send()
    swap_meta.wait_send()

    def sent(v, carry):
        for n in range(3):
            share_out(0, v, n).wait_send()

        @pl.when(core == 0)
        def _():
            @pl.when(y_hi == 0)
            def _():
                transit_copy(v).wait_send()

        entry_out(transit.at[v], v).wait_send()

        @pl.when(core == 1)
        def _():
            entry_on(v).wait_send()
            for n in range(3):
                share_out(1, v, n).wait_send()
                direct(v, n).wait_send()

        return carry

    lax.fori_loop(0, VECS, sent, 0)

    table = jnp.zeros((8, LANES), jnp.float32)
    for n in range(8):
        table = jnp.where(row == n, plane[(n // 2) * 4 + y_hi * 2 + n % 2], table)
    mate = jnp.zeros((8, LANES), jnp.float32)
    for i in range(WALKERS_DEV):
        found = (row == partner[i] // (WALKERS_DEV * 32)) & (lane == core * 4 + (partner[i] & 3))
        value = jnp.sum(pick(found, table), axis=0, keepdims=True)
        mate = jnp.where(row % 4 == i, value, mate)
    paired = 0.5 * (weight + mate)

    some_line = line.at[pl.ds(0, 7)]
    remote(some_line, some_line, line_sem.at[0], line_sem.at[1], sibling).wait_recv()
    summed = line[0]
    for n in range(1, 8):
        summed = summed + line[n]
    top = jnp.broadcast_to(summed, (8, LANES))
    mean = pick(lane == 9, top) / pick(lane == 8, top)
    eye = (row == lane) | (row == lane + 4)
    keep = eye & mine

    def along(values):
        return jnp.sum(jnp.where(keep, values, 0.0), axis=0, keepdims=True)

    biases = jnp.where(core == 0, full[0:4], full[4:8])
    out[0:4, :] = jnp.where(is_bias[0:4], biases, 0.0)
    out[4:5, :] = along(paired)
    out[5:6, :] = along(energy)
    out[6:7, :] = mean[0:1] + jnp.zeros((1, LANES), jnp.float32)

    remote(some_line, some_line, line_sem.at[0], line_sem.at[1], sibling).wait_send()


def deal(tile, paired, energy, bias, mean):
    bias[...] = tile[0:WALKERS_DEV, 0:STOPS * VECS]
    paired[...] = tile[4, 0:WALKERS_DEV]
    energy[...] = tile[5, 0:WALKERS_DEV]
    mean[...] = tile[6, 0:1]


def body(chol, green, fields, weights_in, partner, counts):
    anywhere = pl.BlockSpec(memory_space=pl.ANY)
    vmem = pl.BlockSpec(memory_space=pltpu.VMEM)
    dma = pltpu.SemaphoreType.DMA
    tile = pltpu.VMEM((8, LANES), jnp.float32)
    out = pl.pallas_call(
        kernel,
        out_shape=jax.ShapeDtypeStruct((8, LANES), jnp.float32),
        in_specs=[anywhere] * 5 + [pl.BlockSpec(memory_space=pltpu.SMEM)],
        out_specs=vmem,
        scratch_shapes=[
            pltpu.VMEM((WALKERS_DEV, STOPS * VECS), jnp.float32),
            pltpu.SMEM((WALKERS_DEV,), jnp.float32),
            pltpu.SMEM((WALKERS_DEV,), jnp.int32),
            pltpu.VMEM((3, VECS, NOCC, ORB), jnp.bfloat16),
            pltpu.VMEM((2 * WALKERS_DEV, ORB, NOCC), jnp.bfloat16),
            pltpu.VMEM((NOCC, NOCC), jnp.float32),
            pltpu.VMEM((VECS, QUARTER, ORB), jnp.bfloat16),
            pltpu.VMEM((2 * VECS, 8, LANES), jnp.float32),
            pltpu.VMEM((8, 8, LANES), jnp.float32),
            tile, tile, tile, tile,
            pltpu.VMEM((16, 1, LANES), jnp.float32),
            pltpu.VMEM((8, 1, LANES), jnp.float32),
            dma((3,)), dma((2,)), dma((2,)), dma((2,)), dma((2,)),
            dma((2, VECS)), dma((2, VECS)), dma((VECS,)), dma((VECS,)),
            dma((2, VECS, 3)), dma((2, VECS, 3)), dma((VECS, 3)), dma((VECS, 3)),
            dma((2,)), dma((2,)), pltpu.SemaphoreType.REGULAR((3,)),
        ],
        compiler_params=pltpu.CompilerParams(
            collective_id=0, has_side_effects=True, vmem_limit_bytes=62 * 2**20
        ),
        name="walkers",
    )(chol, green, fields, weights_in, partner, counts)
    results = pl.pallas_call(
        deal,
        out_shape=(
            jax.ShapeDtypeStruct((WALKERS_DEV,), jnp.float32),
            jax.ShapeDtypeStruct((WALKERS_DEV,), jnp.float32),
            jax.ShapeDtypeStruct((WALKERS_DEV, STOPS * VECS), jnp.float32),
            jax.ShapeDtypeStruct((1,), jnp.float32),
        ),
        in_specs=[vmem],
        out_specs=(vmem,) * 4,
        name="deal",
    )(out)
    return results[0], results[1], results[2], results[3].reshape(())


def solution(mesh):
    placed = (
        P("ham", None, None),
        P(("walk", "ham"), None, None),
        P(("walk", "ham"), None),
        P(("walk", "ham")),
        P(("walk", "ham")),
        P("walk", "ham"),
    )
    return jax.shard_map(
        body,
        mesh=mesh,
        in_specs=placed,
        out_specs=(P(("walk", "ham")), P(("walk", "ham")), P(("walk", "ham"), None), P()),
        check_vma=False,
    )
```
